32 devices in a mesh: ctx: 16 (over z, x, core), batch: 2 (over y).
Axes of the slice: x: 2, y: 2, z: 4, core: 2. Of those that a mesh axis runs over, the one named last changes fastest.
Arguments:
- queries: bfloat16 [2, 8192, 256], P('batch', 'ctx')
- keys: bfloat16 [2, 8192, 256], P('batch', 'ctx'), may hold values from -6 to 6
- values: bfloat16 [2, 8192, 256], P('batch', 'ctx'), may hold values from -6 to 6
- output_weight: bfloat16 [256, 512], replicated, may hold values from -0.375 to 0.375
- output_grad: bfloat16 [2, 8192, 512], P('batch', 'ctx'), may hold values from -6 to 6
- rand_blocks: int32 [2, 128, 3], P('batch', 'ctx'), may hold values from 0 to 127, as said below
- glob_pos: int32 [2, 256], P('batch'), may hold values from 0 to 8191, as said below
Outputs:
- attended: bfloat16 [2, 8192, 512], P('batch', 'ctx')
- grad_queries: bfloat16 [2, 8192, 256], P('batch', 'ctx')
- grad_keys: bfloat16 [2, 8192, 256], P('batch', 'ctx')
- grad_values: bfloat16 [2, 8192, 256], P('batch', 'ctx')
- grad_weight: float32 [256, 512], replicated
The draws below stay inside these ranges and needn't reach their ends.
Inputs may be any that keep to these rules, and one draw needn't show every extreme that they name: `rand_blocks`: blocks b and c lie in the same range when b // 8 == c // 8. The 24 numbers of one range of query blocks name at most 2 blocks of any one range; in every sequence there is a range of which every range of query blocks names exactly 2 blocks. `glob_pos`: the positions of one sequence are distinct.
All inputs are finite; a program needn't handle non-finite values.
Results may differ from the reference program's by a relative error of at most 0.0096.
Values may be sent and summed in bfloat16 or wider, within the bound.
No kernel may reach another device: no remote copies, remote signals or barrier semaphores. Data moves between devices by JAX's collectives and lax.ppermute only.
A program may use at most 128 MiB of HBM per device.

```python
import jax
import jax.numpy as jnp
from jax import lax

BLK = 64
HEADS = 4
HDIM = 64
D = 512
RAND = 3
GLOB = 256
QBLK = 8
SEQ = 8192
NBLK = 128
HD = 256
SEQS = 2
CAP = 2
N_CTX = 16


def draw_queries(key, part):
    base = jax.random.truncated_normal(key, -5.0, 5.0, (SEQS, SEQ, HD), jnp.float32)
    return base.astype(jnp.bfloat16)


def draw_rand_blocks(key, part):
    pool_size = N_CTX * CAP
    requests = QBLK * RAND
    entry = jnp.arange(pool_size, dtype=jnp.int32)
    favored_dev = jax.random.randint(jax.random.fold_in(key, 1), (SEQS, 1, 1), 0, N_CTX)
    noise = jax.random.randint(jax.random.fold_in(key, 2), (SEQS, N_CTX, pool_size), 1, 2 ** 20)
    favored = (entry % N_CTX)[None, None, :] == favored_dev
    score = jnp.where(favored, entry[None, None, :], noise * pool_size + entry[None, None, :])
    picked = jnp.argsort(score, axis=-1, stable=True)[..., :requests].astype(jnp.int32)
    owner_dev = picked % N_CTX
    local_block = jax.random.randint(jax.random.fold_in(key, 3), (SEQS, N_CTX, requests), 0, QBLK)
    block_ids = owner_dev * QBLK + local_block
    return block_ids.reshape(SEQS, NBLK, RAND).astype(jnp.int32)


def draw_glob_pos(key, part):
    seq_keys = jax.random.split(key, SEQS)
    chosen = jax.vmap(lambda one_key: jax.random.permutation(one_key, SEQ)[:GLOB])(seq_keys)
    return chosen.astype(jnp.int32)


def steps_of(stream_key, shape, shards, low, top_value):
    level = 1.0
    for axis_at, blocks in shards:
        heights = jax.random.uniform(jax.random.fold_in(jax.random.fold_in(stream_key, 6), axis_at), (blocks,), jnp.float32, low / len(shards), top_value / len(shards))
        level = level * jnp.repeat(jnp.exp(heights), shape[axis_at] // blocks).reshape((-1,) + (1,) * (len(shape) - 1 - axis_at))
    return level


def normal_values(stream_key, shape, deviation, most, cuts=(), kind=jnp.bfloat16):
    gain = steps_of(stream_key, shape, cuts, -0.22, 0.18) if cuts else 1.0
    values = jax.random.normal(stream_key, shape, jnp.float32) * deviation * gain
    return jnp.minimum(jnp.maximum(values, -most), most).astype(kind)


def setup_inputs(seed: int = 0) -> dict:
    key_list = jax.random.split(jax.random.key(seed), 8)
    queries = draw_queries(jax.random.fold_in(key_list[7], 71), 0)
    keys = normal_values(key_list[1], (SEQS, SEQ, HD), 1.0, 6.0, ((0, 2), (1, 16)))
    values = normal_values(key_list[2], (SEQS, SEQ, HD), 1.0, 6.0, ((0, 2), (1, 16)))
    output_weight = normal_values(key_list[3], (HD, D), HD ** -0.5, 0.375)
    output_grad = normal_values(key_list[4], (SEQS, SEQ, D), 1.0, 6.0, ((0, 2), (1, 16)))
    rand_blocks = draw_rand_blocks(jax.random.fold_in(key_list[7], 71), 0)
    glob_pos = draw_glob_pos(jax.random.fold_in(key_list[7], 71), 0)
    return dict(queries=queries, keys=keys, values=values, output_weight=output_weight, output_grad=output_grad, rand_blocks=rand_blocks, glob_pos=glob_pos)


def product(form, left, right):
    return jnp.einsum(form, left.astype(jnp.float32), right.astype(jnp.float32), precision=lax.Precision.HIGHEST)


def attend(query_group, local_keys, local_values, glob_keys, glob_values, grad_group, score_scale):
    scores_local = product("nqhd,nkhd->nhqk", query_group, local_keys) * score_scale
    scores_glob = product("nqhd,khd->nhqk", query_group, glob_keys) * score_scale
    row_max = jnp.maximum(jnp.max(scores_local, axis=-1, keepdims=True), jnp.max(scores_glob, axis=-1, keepdims=True))
    expo_local = jnp.exp(scores_local - row_max)
    expo_glob = jnp.exp(scores_glob - row_max)
    denominator = jnp.sum(expo_local, axis=-1, keepdims=True) + jnp.sum(expo_glob, axis=-1, keepdims=True)
    probs_local = expo_local / denominator
    probs_glob = expo_glob / denominator
    probs_local16 = probs_local.astype(jnp.bfloat16)
    probs_glob16 = probs_glob.astype(jnp.bfloat16)
    attention = product("nhqk,nkhd->nqhd", probs_local16, local_values) + product("nhqk,khd->nqhd", probs_glob16, glob_values)
    vgrad_local = product("nhqk,nqhd->nkhd", probs_local16, grad_group)
    vgrad_glob = product("nhqk,nqhd->khd", probs_glob16, grad_group)
    dprob_local = product("nqhd,nkhd->nhqk", grad_group, local_values)
    dprob_glob = product("nqhd,khd->nhqk", grad_group, glob_values)
    delta = jnp.swapaxes(jnp.sum(grad_group.astype(jnp.float32) * attention, axis=-1), 1, 2)[..., None]
    dscore_local = (probs_local * (dprob_local - delta) * score_scale).astype(jnp.bfloat16)
    dscore_glob = (probs_glob * (dprob_glob - delta) * score_scale).astype(jnp.bfloat16)
    grad_query = product("nhqk,nkhd->nqhd", dscore_local, local_keys) + product("nhqk,khd->nqhd", dscore_glob, glob_keys)
    kgrad_local = product("nhqk,nqhd->nkhd", dscore_local, query_group)
    kgrad_glob = product("nhqk,nqhd->khd", dscore_glob, query_group)
    return attention, grad_query, kgrad_local, vgrad_local, kgrad_glob, vgrad_glob


def one_sequence(query_rows, key_rows, value_rows, grad_rows, output_weight, blocks_of, positions):
    nblocks = SEQ // BLK
    groups = nblocks // 8
    span = (3 + RAND) * BLK
    score_scale = HDIM ** -0.5
    key_value = jnp.concatenate([key_rows, value_rows], axis=1)
    grad_attn = jnp.dot(grad_rows, output_weight.T, preferred_element_type=jnp.float32).astype(jnp.bfloat16)
    padded_blocks = key_value.reshape(nblocks, BLK, 2 * HD)
    glob_pair = jnp.take(key_value, positions, axis=0)
    glob_keys = glob_pair[:, :HD].reshape(GLOB, HEADS, HDIM)
    glob_values = glob_pair[:, HD:].reshape(GLOB, HEADS, HDIM)
    query_groups = query_rows.reshape(groups, 8, BLK, HEADS, HDIM)
    grad_groups = grad_attn.reshape(groups, 8, BLK, HEADS, HDIM)

    def group_step(carried, inputs):
        window_sum, glob_sum = carried
        group_index, query_group, grad_group = inputs
        first_block = group_index * 8
        block_ids = first_block + jnp.arange(8).astype(jnp.int32)
        win_ids = ((block_ids[:, None] + jnp.arange(3).astype(jnp.int32)[None, :] - 1) % nblocks).astype(jnp.int32)
        rand_ids = lax.dynamic_slice_in_dim(blocks_of, first_block, 8, 0).astype(jnp.int32)
        all_ids = jnp.concatenate([win_ids, rand_ids], axis=1)
        local_pair = jnp.take(padded_blocks, all_ids, axis=0).reshape(8, span, 2 * HD)
        local_keys = local_pair[..., :HD].reshape(8, span, HEADS, HDIM)
        local_values = local_pair[..., HD:].reshape(8, span, HEADS, HDIM)
        attention, grad_query, kgrad_local, vgrad_local, kgrad_glob, vgrad_glob = attend(
            query_group, local_keys, local_values, glob_keys, glob_values, grad_group, score_scale)
        local_grads = jnp.concatenate([kgrad_local.reshape(8, span, HD), vgrad_local.reshape(8, span, HD)], axis=2)
        local_grads = local_grads.reshape(8, 3 + RAND, BLK, 2 * HD)
        rounded = lax.optimization_barrier(local_grads[:, 3:].astype(jnp.bfloat16)).astype(jnp.float32)
        window_sum = window_sum.at[win_ids].add(local_grads[:, :3])
        window_sum = window_sum.at[rand_ids].add(rounded)
        glob_sum = glob_sum + jnp.concatenate([kgrad_glob.reshape(GLOB, HD), vgrad_glob.reshape(GLOB, HD)], axis=1)
        return (window_sum, glob_sum), (attention.astype(jnp.bfloat16), grad_query.astype(jnp.bfloat16))

    start_state = (jnp.zeros((nblocks, BLK, 2 * HD), jnp.float32), jnp.zeros((GLOB, 2 * HD), jnp.float32))
    (window_sum, glob_sum), (attention, grad_query) = lax.scan(
        group_step, start_state, (jnp.arange(groups).astype(jnp.int32), query_groups, grad_groups))
    grand_total = window_sum.reshape(SEQ, 2 * HD).at[positions].add(glob_sum)
    attention_rows = attention.reshape(SEQ, HD)
    attended = jnp.dot(attention_rows, output_weight, preferred_element_type=jnp.float32).astype(jnp.bfloat16)
    weight_term = jnp.dot(attention_rows.T, grad_rows, preferred_element_type=jnp.float32)
    return (attended, grad_query.reshape(SEQ, HD), grand_total[:, :HD].astype(jnp.bfloat16),
            grand_total[:, HD:].astype(jnp.bfloat16), weight_term)


def reference(queries, keys, values, output_weight, output_grad, rand_blocks, glob_pos):
    results = []
    grad_weight = jnp.zeros((HD, D), jnp.float32)
    for sequence in range(SEQS):
        outcome = one_sequence(queries[sequence], keys[sequence], values[sequence], output_grad[sequence],
                               output_weight, rand_blocks[sequence], glob_pos[sequence])
        results.append(outcome[:4])
        grad_weight = grad_weight + outcome[4]
    attended = jnp.stack([entry[0] for entry in results])
    grad_queries = jnp.stack([entry[1] for entry in results])
    grad_keys = jnp.stack([entry[2] for entry in results])
    grad_values = jnp.stack([entry[3] for entry in results])
    return (attended, grad_queries, grad_keys, grad_values, grad_weight)
```

```python
import functools

import jax
import jax.numpy as jnp
from jax import lax
from jax.experimental import pallas as pl
from jax.experimental.pallas import tpu as pltpu
from jax.sharding import PartitionSpec as P

BLK = 64
HEADS = 4
RAND = 3
LANES = 128
MIB = 1024 * 1024
LOG2E = 1.4426950408889634

F32 = jnp.float32
BF16 = jnp.bfloat16
VMEM = pl.BlockSpec(memory_space=pltpu.VMEM)
SMEM = pl.BlockSpec(memory_space=pltpu.SMEM)


def params(mib):
    return pltpu.CompilerParams(vmem_limit_bytes=mib * MIB)


def dot(left, right, over_left, over_right):
    return lax.dot_general(
        left, right, (((over_left,), (over_right,)), ((), ())), preferred_element_type=F32
    )


def ask_kernel(span_devices, capacity, first_ref, want_ref, pos_ref, k_ref, v_ref,
               send_ref, slot_ref, count_ref, list_ref):
    tokens, width = k_ref.shape
    glob = pos_ref.shape[1]
    query_blocks = tokens // BLK
    rows = glob // span_devices
    for dev in range(span_devices):
        count_ref[dev] = 0
        for slot in range(capacity):
            list_ref[dev * capacity + slot] = -1

    def request(at, carry):
        wanted = want_ref[at]
        owner = lax.div(wanted, query_blocks)
        slot = owner * capacity + jnp.minimum(count_ref[owner], capacity - 1)
        count_ref[owner] = count_ref[owner] + 1
        list_ref[slot] = wanted - owner * query_blocks
        slot_ref[at] = slot
        return carry

    lax.fori_loop(0, query_blocks * RAND, request, 0)
    here = first_ref[0] + lax.broadcasted_iota(jnp.int32, (tokens, glob), 0)
    owned = jnp.where(here == pos_ref[...], 1.0, 0.0).astype(BF16)
    send_ref[:, :width] = dot(owned, k_ref[...], 0, 0).astype(BF16)
    send_ref[:, width : 2 * width] = dot(owned, v_ref[...], 0, 0).astype(BF16)
    row = lax.broadcasted_iota(jnp.int32, (glob, LANES), 0)
    lane = lax.broadcasted_iota(jnp.int32, (glob, LANES), 1)
    listed = jnp.full((glob, LANES), -1, jnp.int32)
    for dev in range(span_devices):
        mine = (row >= dev * rows) & (row < (dev + 1) * rows)
        for slot in range(capacity):
            listed = jnp.where(mine & (lane == slot), list_ref[dev * capacity + slot], listed)
    send_ref[:, 2 * width :] = listed.astype(F32).astype(BF16)


def reply_kernel(span_devices, capacity, got_ref, k_ref, v_ref, out_ref, glob_ref, asked_ref,
                 asked_smem, sem):
    tokens, width = k_ref.shape
    glob = got_ref.shape[0]
    rows = glob // span_devices
    source = lax.broadcasted_iota(jnp.int32, (span_devices, glob), 1)
    target = lax.broadcasted_iota(jnp.int32, (span_devices, glob), 0)
    pick = jnp.where(source == target * rows, 1.0, 0.0).astype(BF16)
    asked_ref[...] = dot(pick, got_ref[:, 2 * width :], 1, 0).astype(jnp.int32)
    copy = pltpu.make_async_copy(asked_ref, asked_smem, sem)
    copy.start()
    source = lax.broadcasted_iota(jnp.int32, (rows, glob), 1)
    target = lax.broadcasted_iota(jnp.int32, (rows, glob), 0)
    total = jnp.where(lax.rem(source, rows) == target, 1.0, 0.0).astype(BF16)
    glob_ref[...] = dot(total, got_ref[:, : 2 * width], 1, 0).astype(BF16)
    copy.wait()
    for dev in range(span_devices):
        for slot in range(capacity):
            block = jnp.maximum(asked_smem[dev, slot], 0)
            source = pl.ds(pl.multiple_of(block * BLK, BLK), BLK)
            target = pl.ds((dev * capacity + slot) * BLK, BLK)
            out_ref[target, :width] = k_ref[source, :]
            out_ref[target, width:] = v_ref[source, :]


def attend_kernel(slot_ref, q_ref, ga_ref, og_ref, k_ref, v_ref, low_ref, high_ref, glob_ref, arr_ref,
                  out_ref, red_ref, inner_ref, elow_ref, ehigh_ref, att_ref, dq_ref,
                  pad_ref, kc_ref, vc_ref, acc_ref, gacc_ref):
    tokens, width = q_ref.shape
    query_blocks = tokens // BLK
    head_size = width // HEADS
    scale = head_size ** (-0.5)
    win, local = 3 * BLK, (3 + RAND) * BLK
    pad_ref[:BLK] = low_ref[...]
    pad_ref[BLK : BLK + tokens, :width] = k_ref[...]
    pad_ref[BLK : BLK + tokens, width:] = v_ref[...]
    pad_ref[BLK + tokens :] = high_ref[...]
    kc_ref[local:] = glob_ref[:, :width]
    vc_ref[local:] = glob_ref[:, width:]
    acc_ref[...] = jnp.zeros_like(acc_ref)
    gacc_ref[...] = jnp.zeros_like(gacc_ref)
    row_head = lax.broadcasted_iota(jnp.int32, (HEADS * BLK, width), 0) // BLK
    lane_head = lax.broadcasted_iota(jnp.int32, (HEADS * BLK, width), 1) // head_size
    mask = jnp.where(row_head == lane_head, 1.0, 0.0).astype(BF16)
    keep = jnp.where(row_head == lane_head, 1.0, 0.0)

    def by_head(rows):
        return jnp.concatenate([rows] * HEADS, axis=0) * mask

    def own_head(full):
        kept = full * keep
        return sum(kept[h * BLK : (h + 1) * BLK] for h in range(HEADS))

    def one_block(i, carry):
        base = pl.multiple_of(i * BLK, BLK)
        slots = []
        kc_ref[:win] = pad_ref[pl.ds(base, win), :width]
        vc_ref[:win] = pad_ref[pl.ds(base, win), width:]
        for j in range(RAND):
            slot = pl.ds(pl.multiple_of(slot_ref[i * RAND + j] * BLK, BLK), BLK)
            slots.append(slot)
            kc_ref[win + j * BLK : win + (j + 1) * BLK] = arr_ref[slot, :width]
            vc_ref[win + j * BLK : win + (j + 1) * BLK] = arr_ref[slot, width:]
        q_by_head = by_head(q_ref[pl.ds(base, BLK), :])
        ga_by_head = by_head(ga_ref[pl.ds(base, BLK), :])
        scores = dot(kc_ref[...], q_by_head, 1, 1) * (scale * LOG2E)
        expo = jnp.exp2(scores - jnp.max(scores, axis=0, keepdims=True))
        probs = expo * (1.0 / jnp.sum(expo, axis=0, keepdims=True))
        probs16 = probs.astype(BF16)
        dprobs = dot(vc_ref[...], ga_by_head, 1, 1)
        delta = jnp.sum(probs16.astype(F32) * dprobs, axis=0, keepdims=True)
        dscores = (probs * (dprobs - delta) * scale).astype(BF16)
        att_ref[pl.ds(base, BLK), :] = own_head(dot(probs16, vc_ref[...], 0, 0)).astype(BF16)
        dq_ref[pl.ds(base, BLK), :] = own_head(dot(dscores, kc_ref[...], 0, 0)).astype(BF16)
        for part, terms in (
            (slice(0, width), dot(dscores, q_by_head, 1, 0)),
            (slice(width, 2 * width), dot(probs16, ga_by_head, 1, 0)),
        ):
            acc_ref[pl.ds(base, win), part] += terms[:win]
            gacc_ref[:, part] += terms[local:]
            for j in range(RAND):
                out_ref[slots[j], part] = terms[win + j * BLK : win + (j + 1) * BLK].astype(BF16)
        return carry

    lax.fori_loop(0, query_blocks, one_block, 0)
    inner_ref[...] = acc_ref[BLK : BLK + tokens]
    elow_ref[...] = acc_ref[:BLK].astype(BF16)
    ehigh_ref[...] = acc_ref[BLK + tokens :].astype(BF16)
    red_ref[:, : 2 * width] = gacc_ref[...].astype(BF16)
    red_ref[:, 2 * width :] = dot(att_ref[...], og_ref[...], 0, 0).astype(BF16)


def share_kernel(span_devices, got_ref, glob_ref, weight_ref):
    count, width = got_ref.shape
    rows = count // span_devices
    source = lax.broadcasted_iota(jnp.int32, (rows, count), 1)
    target = lax.broadcasted_iota(jnp.int32, (rows, count), 0)
    total = jnp.where(lax.rem(source, rows) == target, 1.0, 0.0).astype(BF16)
    part = glob_ref.shape[1]
    glob_ref[...] = dot(total, got_ref[:, :part], 1, 0).astype(BF16)
    weight_ref[...] = dot(total, got_ref[:, part:], 1, 0)


def finish_kernel(span_devices, capacity, first_ref, asked_ref, pos_ref, back_ref, inner_ref,
                  from_low_ref, from_high_ref, glob_ref, dk_ref, dv_ref, acc_ref):
    tokens, width = dk_ref.shape
    glob = glob_ref.shape[0]
    here = first_ref[0] + lax.broadcasted_iota(jnp.int32, (tokens, glob), 0)
    owned = jnp.where(here == pos_ref[...], 1.0, 0.0).astype(BF16)
    acc_ref[...] = inner_ref[...] + dot(owned, glob_ref[...], 1, 0)
    acc_ref[:BLK] += from_low_ref[...].astype(F32)
    acc_ref[tokens - BLK :] += from_high_ref[...].astype(F32)
    for dev in range(span_devices):
        for slot in range(capacity):
            block = asked_ref[dev, slot]

            @pl.when(block >= 0)
            def _():
                rows = pl.ds(pl.multiple_of(block * BLK, BLK), BLK)
                at = (dev * capacity + slot) * BLK
                acc_ref[rows, :] += back_ref[at : at + BLK, :].astype(F32)

    dk_ref[...] = acc_ref[:, :width].astype(BF16)
    dv_ref[...] = acc_ref[:, width:].astype(BF16)


def shards(queries, keys, values, output_weight, output_grad, rand_blocks, glob_pos):
    q, k, v, og = queries[0], keys[0], values[0], output_grad[0]
    tokens, width = q.shape
    model = og.shape[1]
    glob = glob_pos.shape[1]
    query_blocks = tokens // BLK
    span = lax.axis_size("ctx")
    batch = lax.axis_size("batch")
    requests = query_blocks * RAND
    capacity = requests // span + 1
    slots = span * capacity
    rows = glob // span
    first = (lax.axis_index("ctx") * tokens).astype(jnp.int32).reshape(1)
    shape = jax.ShapeDtypeStruct
    forward = [(i, (i + 1) % span) for i in range(span)]
    backward = [(target, source) for source, target in forward]

    def swap(x):
        return lax.all_to_all(x, "ctx", split_axis=0, concat_axis=0, tiled=True)

    send, slot_index = pl.pallas_call(
        functools.partial(ask_kernel, span, capacity),
        name="ask",
        out_shape=(shape((glob, 2 * width + LANES), BF16), shape((requests,), jnp.int32)),
        in_specs=[SMEM, SMEM, VMEM, VMEM, VMEM],
        out_specs=(VMEM, SMEM),
        scratch_shapes=[pltpu.SMEM((span,), jnp.int32), pltpu.SMEM((slots,), jnp.int32)],
        compiler_params=params(16),
    )(first, rand_blocks.reshape(requests), glob_pos, k, v)
    got = swap(send)
    key_value_edges = [
        jnp.concatenate([k[edge], v[edge]], axis=1)
        for edge in (slice(tokens - BLK, tokens), slice(0, BLK))
    ]
    low = lax.ppermute(key_value_edges[0], "ctx", forward)
    high = lax.ppermute(key_value_edges[1], "ctx", backward)
    grad_attn = dot(og, output_weight, 1, 1).astype(BF16)

    reply, glob_mine, asked = pl.pallas_call(
        functools.partial(reply_kernel, span, capacity),
        name="reply",
        out_shape=(
            shape((slots * BLK, 2 * width), BF16),
            shape((rows, 2 * width), BF16),
            shape((span, LANES), jnp.int32),
        ),
        in_specs=[VMEM] * 3,
        out_specs=(VMEM,) * 3,
        scratch_shapes=[pltpu.SMEM((span, LANES), jnp.int32), pltpu.SemaphoreType.DMA],
        compiler_params=params(16),
    )(got, k, v)
    arrived = swap(reply)
    glob_rows = lax.all_gather(glob_mine, "ctx", axis=0, tiled=True)

    block = (3 + RAND) * BLK + glob
    outgoing, reduce_terms, inner, edge_low, edge_high, attention_rows, grad_queries = pl.pallas_call(
        attend_kernel,
        name="attend",
        out_shape=(
            shape((slots * BLK, 2 * width), BF16),
            shape((glob, 2 * width + model), BF16),
            shape((tokens, 2 * width), F32),
            shape((BLK, 2 * width), BF16),
            shape((BLK, 2 * width), BF16),
            shape((tokens, width), BF16),
            shape((tokens, width), BF16),
        ),
        in_specs=[SMEM] + [VMEM] * 9,
        out_specs=(VMEM,) * 7,
        scratch_shapes=[
            pltpu.VMEM((tokens + 2 * BLK, 2 * width), BF16),
            pltpu.VMEM((block, width), BF16),
            pltpu.VMEM((block, width), BF16),
            pltpu.VMEM((tokens + 2 * BLK, 2 * width), F32),
            pltpu.VMEM((glob, 2 * width), F32),
        ],
        compiler_params=params(32),
    )(slot_index, q, grad_attn, og, k, v, low, high, glob_rows, arrived)

    reduced = swap(reduce_terms)
    back = swap(outgoing)
    from_high = lax.ppermute(edge_low, "ctx", backward)
    from_low = lax.ppermute(edge_high, "ctx", forward)
    glob_share, weight_share = pl.pallas_call(
        functools.partial(share_kernel, span),
        name="share",
        out_shape=(shape((rows, 2 * width), BF16), shape((rows, model), F32)),
        in_specs=[VMEM],
        out_specs=(VMEM,) * 2,
        compiler_params=params(16),
    )(reduced)
    weight_sum = weight_share
    for step in range(1, batch):
        weight_sum = weight_sum + lax.ppermute(
            weight_share, "batch", [(i, (i + step) % batch) for i in range(batch)]
        )
    glob_total = lax.all_gather(glob_share, "ctx", axis=0, tiled=True)
    grad_weight = lax.all_gather(weight_sum, "ctx", axis=0, tiled=True)
    attended = dot(attention_rows, output_weight, 1, 0).astype(BF16)

    grad_keys, grad_values = pl.pallas_call(
        functools.partial(finish_kernel, span, capacity),
        name="finish",
        out_shape=(shape((tokens, width), BF16), shape((tokens, width), BF16)),
        in_specs=[SMEM, SMEM] + [VMEM] * 6,
        out_specs=(VMEM,) * 2,
        scratch_shapes=[pltpu.VMEM((tokens, 2 * width), F32)],
        compiler_params=params(24),
    )(first, asked, glob_pos, back, inner, from_low, from_high, glob_total)
    return (
        attended[None],
        grad_queries[None],
        grad_keys[None],
        grad_values[None],
        grad_weight,
    )


def solution(mesh):
    in_specs = (
        P("batch", "ctx", None),
        P("batch", "ctx", None),
        P("batch", "ctx", None),
        P(),
        P("batch", "ctx", None),
        P("batch", "ctx", None),
        P("batch", None),
    )
    out_specs = (
        P("batch", "ctx", None),
        P("batch", "ctx", None),
        P("batch", "ctx", None),
        P("batch", "ctx", None),
        P(),
    )
    return jax.shard_map(shards, mesh=mesh, in_specs=in_specs, out_specs=out_specs, check_vma=False)
```

```python
import functools

import jax
import jax.numpy as jnp
from jax import lax
from jax.experimental import pallas as pl
from jax.experimental.pallas import tpu as pltpu
from jax.sharding import PartitionSpec as P

BLK = 64
HEADS = 4
RAND = 3
LANES = 128
MIB = 1024 * 1024
LOG2E = 1.4426950408889634

F32 = jnp.float32
BF16 = jnp.bfloat16
VMEM = pl.BlockSpec(memory_space=pltpu.VMEM)
SMEM = pl.BlockSpec(memory_space=pltpu.SMEM)


def params(mib):
    return pltpu.CompilerParams(vmem_limit_bytes=mib * MIB)


def dot(left, right, over_left, over_right):
    return lax.dot_general(
        left, right, (((over_left,), (over_right,)), ((), ())), preferred_element_type=F32
    )


def ask_kernel(half, capacity, strides, here_ref, want_ref, pos_ref, k_ref, v_ref,
               send_ref, place_ref, count_ref, list_ref):
    tokens, width = k_ref.shape
    glob = pos_ref.shape[1]
    query_blocks = tokens // BLK
    requests = query_blocks * RAND
    rows = glob // half
    lists = 2 * capacity
    me = here_ref[0]
    my_half = lax.div(me, half)
    for entry in range(2 * half):
        count_ref[entry] = 0
    for entry in range(half * lists):
        list_ref[entry] = -1

    def request(at, carry):
        wanted = want_ref[at]
        owner = lax.div(wanted, query_blocks)
        rank = jnp.minimum(count_ref[owner], capacity - 1)
        count_ref[owner] = count_ref[owner] + 1
        owner_half = lax.div(owner, half)
        member = owner - owner_half * half
        slot = jnp.where(owner_half == my_half, 0, capacity) + rank
        list_ref[member * lists + slot] = wanted - owner * query_blocks
        for use in range(3):
            place_ref[use * requests + at] = member * strides[use] + slot * BLK
        return carry

    lax.fori_loop(0, requests, request, 0)
    here = me * tokens + lax.broadcasted_iota(jnp.int32, (tokens, glob), 0)
    owned = jnp.where(here == pos_ref[...], 1.0, 0.0).astype(BF16)
    send_ref[:, :width] = dot(owned, k_ref[...], 0, 0).astype(BF16)
    send_ref[:, width : 2 * width] = dot(owned, v_ref[...], 0, 0).astype(BF16)
    lane = lax.broadcasted_iota(jnp.int32, (rows, LANES), 1)
    for member in range(half):
        listed = jnp.full((rows, LANES), -1, jnp.int32)
        for slot in range(lists):
            listed = jnp.where(lane == slot, list_ref[member * lists + slot], listed)
        send_ref[member * rows : (member + 1) * rows, 2 * width :] = listed.astype(F32).astype(BF16)


def heard_kernel(half, got_ref, glob_ref, asked_ref):
    glob = got_ref.shape[0]
    rows = glob // half
    wide = glob_ref.shape[1]
    source = lax.broadcasted_iota(jnp.int32, (half, glob), 1)
    target = lax.broadcasted_iota(jnp.int32, (half, glob), 0)
    pick = jnp.where(source == target * rows, 1.0, 0.0).astype(BF16)
    asked_ref[...] = dot(pick, got_ref[:, wide:], 1, 0).astype(jnp.int32)
    source = lax.broadcasted_iota(jnp.int32, (rows, glob), 1)
    target = lax.broadcasted_iota(jnp.int32, (rows, glob), 0)
    total = jnp.where(lax.rem(source, rows) == target, 1.0, 0.0).astype(BF16)
    glob_ref[...] = dot(total, got_ref[:, :wide], 1, 0).astype(BF16)


def reply_kernel(half, capacity, asked_ref, k_ref, v_ref, mk_ref, mv_ref, glob_ref, mglob_ref, out_ref):
    tokens, width = k_ref.shape
    stride = out_ref.shape[0] // half
    share = (glob_ref[...].astype(F32) + mglob_ref[...].astype(F32)).astype(BF16)
    for member in range(half):
        for slot in range(2 * capacity):
            block = jnp.maximum(asked_ref[member, slot], 0)
            source = pl.ds(pl.multiple_of(block * BLK, BLK), BLK)
            target = pl.ds(member * stride + slot * BLK, BLK)
            own = slot < capacity
            out_ref[target, :width] = (k_ref if own else mk_ref)[source, :]
            out_ref[target, width:] = (v_ref if own else mv_ref)[source, :]
        out_ref[member * stride + 2 * capacity * BLK : (member + 1) * stride, :] = share


def attend_kernel(half, capacity, place_ref, q_ref, ga_ref, og_ref, k_ref, v_ref, low_ref, high_ref, arr_ref,
                  dk_out_ref, dv_out_ref, inner_k_ref, inner_v_ref, elow_ref, ehigh_ref, att_ref, dq_ref,
                  pad_ref, kc_ref, vc_ref, acc_ref, gacc_ref):
    tokens, width = q_ref.shape
    query_blocks = tokens // BLK
    head_size = width // HEADS
    scale = head_size ** (-0.5)
    win, local = 3 * BLK, (3 + RAND) * BLK
    requests = query_blocks * RAND
    pad_ref[:BLK] = low_ref[...]
    pad_ref[BLK : BLK + tokens, :width] = k_ref[...]
    pad_ref[BLK : BLK + tokens, width:] = v_ref[...]
    pad_ref[BLK + tokens :] = high_ref[...]
    skip = 2 * capacity * BLK
    rows = gacc_ref.shape[0] // half
    for member in range(half):
        at = member * (arr_ref.shape[0] // half) + skip
        kc_ref[local + member * rows : local + (member + 1) * rows] = arr_ref[at : at + rows, :width]
        vc_ref[local + member * rows : local + (member + 1) * rows] = arr_ref[at : at + rows, width:]
    acc_ref[...] = jnp.zeros_like(acc_ref)
    gacc_ref[...] = jnp.zeros_like(gacc_ref)
    row_head = lax.broadcasted_iota(jnp.int32, (HEADS * BLK, width), 0) // BLK
    lane_head = lax.broadcasted_iota(jnp.int32, (HEADS * BLK, width), 1) // head_size
    mask = jnp.where(row_head == lane_head, 1.0, 0.0).astype(BF16)
    keep = jnp.where(row_head == lane_head, 1.0, 0.0)

    def by_head(rows):
        return jnp.concatenate([rows] * HEADS, axis=0) * mask

    def own_head(full):
        kept = full * keep
        return sum(kept[h * BLK : (h + 1) * BLK] for h in range(HEADS))

    def one_block(i, carry):
        base = pl.multiple_of(i * BLK, BLK)
        kc_ref[:win] = pad_ref[pl.ds(base, win), :width]
        vc_ref[:win] = pad_ref[pl.ds(base, win), width:]
        for j in range(RAND):
            slot = pl.ds(pl.multiple_of(place_ref[i * RAND + j], BLK), BLK)
            kc_ref[win + j * BLK : win + (j + 1) * BLK] = arr_ref[slot, :width]
            vc_ref[win + j * BLK : win + (j + 1) * BLK] = arr_ref[slot, width:]
        q_by_head = by_head(q_ref[pl.ds(base, BLK), :])
        ga_by_head = by_head(ga_ref[pl.ds(base, BLK), :])
        scores = dot(kc_ref[...], q_by_head, 1, 1) * (scale * LOG2E)
        expo = jnp.exp2(scores - jnp.max(scores, axis=0, keepdims=True))
        probs = expo * (1.0 / jnp.sum(expo, axis=0, keepdims=True))
        probs16 = probs.astype(BF16)
        dprobs = dot(vc_ref[...], ga_by_head, 1, 1)
        delta = jnp.sum(probs16.astype(F32) * dprobs, axis=0, keepdims=True)
        dscores = (probs * (dprobs - delta) * scale).astype(BF16)
        att_ref[pl.ds(base, BLK), :] = own_head(dot(probs16, vc_ref[...], 0, 0)).astype(BF16)
        dq_ref[pl.ds(base, BLK), :] = own_head(dot(dscores, kc_ref[...], 0, 0)).astype(BF16)
        for out_ref, at, part, terms in (
            (dv_out_ref, 1, slice(width, 2 * width), dot(probs16, ga_by_head, 1, 0)),
            (dk_out_ref, 2, slice(0, width), dot(dscores, q_by_head, 1, 0)),
        ):
            acc_ref[pl.ds(base, win), part] += terms[:win]
            gacc_ref[:, part] += terms[local:]
            for j in range(RAND):
                slot = place_ref[at * requests + i * RAND + j]
                out_ref[pl.ds(pl.multiple_of(slot, 16), BLK), :] = terms[
                    win + j * BLK : win + (j + 1) * BLK
                ].astype(BF16)
        return carry

    lax.fori_loop(0, query_blocks, one_block, 0)
    inner_k_ref[...] = acc_ref[BLK : BLK + tokens, :width]
    inner_v_ref[...] = acc_ref[BLK : BLK + tokens, width:]
    elow_ref[...] = acc_ref[:BLK].astype(BF16)
    ehigh_ref[...] = acc_ref[BLK + tokens :].astype(BF16)
    gacc_ref[:, 2 * width :] = dot(att_ref[...], og_ref[...], 0, 0)
    stride = dv_out_ref.shape[0] // half
    for member in range(half):
        for part in range(gacc_ref.shape[1] // width):
            at = member * stride + skip + part * rows
            dv_out_ref[at : at + rows, :] = gacc_ref[
                member * rows : (member + 1) * rows, part * width : (part + 1) * width
            ].astype(BF16)


def fold_kernel(half, capacity, asked_ref, back_ref, inner_ref, own_ref, mirror_ref, *rest):
    stride = back_ref.shape[0] // half
    skip = 2 * capacity * BLK
    mirror_acc = rest[-1]
    own_ref[...] = inner_ref[...]
    mirror_acc[...] = jnp.zeros_like(mirror_acc)
    for member in range(half):
        for slot in range(2 * capacity):
            block = asked_ref[member, slot]
            acc_ref = own_ref if slot < capacity else mirror_acc
            at = member * stride + slot * BLK

            @pl.when(block >= 0)
            def _():
                rows = pl.ds(pl.multiple_of(block * BLK, BLK), BLK)
                acc_ref[rows, :] += back_ref[at : at + BLK, :].astype(F32)

    mirror_ref[...] = mirror_acc[...].astype(BF16)
    if len(rest) > 1:
        share_ref = rest[0]
        rows, wide = share_ref.shape
        width = back_ref.shape[1]
        total = back_ref[skip:stride, :].astype(F32)
        for member in range(1, half):
            total += back_ref[member * stride + skip : (member + 1) * stride, :].astype(F32)
        for part in range(wide // width):
            share_ref[:, part * width : (part + 1) * width] = total[
                part * rows : (part + 1) * rows
            ].astype(BF16)


def finish_kernel(here_ref, pos_ref, own_k_ref, own_v_ref, far_k_ref, far_v_ref, from_low_ref,
                  from_high_ref, glob_ref, dk_ref, dv_ref, acc_ref):
    tokens, width = dk_ref.shape
    glob = glob_ref.shape[0]
    here = here_ref[0] * tokens + lax.broadcasted_iota(jnp.int32, (tokens, glob), 0)
    owned = jnp.where(here == pos_ref[...], 1.0, 0.0).astype(BF16)
    for part, own_ref, far_ref, out_ref in (
        (slice(0, width), own_k_ref, far_k_ref, dk_ref),
        (slice(width, 2 * width), own_v_ref, far_v_ref, dv_ref),
    ):
        acc_ref[...] = own_ref[...] + far_ref[...].astype(F32) + dot(owned, glob_ref[:, part], 1, 0)
        acc_ref[:BLK] += from_low_ref[:, part].astype(F32)
        acc_ref[tokens - BLK :] += from_high_ref[:, part].astype(F32)
        out_ref[...] = acc_ref[...].astype(BF16)


def shards(queries, keys, values, output_weight, output_grad, rand_blocks, glob_pos):
    q, k, v, og = queries[0], keys[0], values[0], output_grad[0]
    tokens, width = q.shape
    model = og.shape[1]
    glob = glob_pos.shape[1]
    query_blocks = tokens // BLK
    span = lax.axis_size("ctx")
    batch = lax.axis_size("batch")
    requests = query_blocks * RAND
    capacity = requests // span + 1
    half = span // 2
    rows = glob // half
    wide = 2 * width + model
    skip = 2 * capacity * BLK
    strides = (skip + rows, skip + rows * wide // width, skip)
    here = lax.axis_index("ctx").astype(jnp.int32).reshape(1)
    shape = jax.ShapeDtypeStruct
    forward = [(i, (i + 1) % span) for i in range(span)]
    backward = [(target, source) for source, target in forward]
    mirror = [(i, (i + half) % span) for i in range(span)]
    halves = [list(range(half)), list(range(half, span))]

    def swap(x):
        return lax.all_to_all(
            x, "ctx", split_axis=0, concat_axis=0, axis_index_groups=halves, tiled=True
        )

    mirror_k = lax.ppermute(k, "ctx", mirror)
    mirror_v = lax.ppermute(v, "ctx", mirror)
    send, places = pl.pallas_call(
        functools.partial(ask_kernel, half, capacity, strides),
        name="ask",
        out_shape=(shape((glob, 2 * width + LANES), BF16), shape((3 * requests,), jnp.int32)),
        in_specs=[SMEM, SMEM, VMEM, VMEM, VMEM],
        out_specs=(VMEM, SMEM),
        scratch_shapes=[pltpu.SMEM((span,), jnp.int32), pltpu.SMEM((span * capacity,), jnp.int32)],
        compiler_params=params(16),
    )(here, rand_blocks.reshape(requests), glob_pos, k, v)
    got = swap(send)
    key_value_edges = [
        jnp.concatenate([k[edge], v[edge]], axis=1)
        for edge in (slice(tokens - BLK, tokens), slice(0, BLK))
    ]
    low = lax.ppermute(key_value_edges[0], "ctx", forward)
    high = lax.ppermute(key_value_edges[1], "ctx", backward)
    grad_attn = dot(og, output_weight, 1, 1).astype(BF16)

    glob_here, asked = pl.pallas_call(
        functools.partial(heard_kernel, half),
        name="heard",
        out_shape=(shape((rows, 2 * width), BF16), shape((half, LANES), jnp.int32)),
        in_specs=[VMEM],
        out_specs=(VMEM,) * 2,
        compiler_params=params(16),
    )(got)
    glob_there = lax.ppermute(glob_here, "ctx", mirror)
    reply = pl.pallas_call(
        functools.partial(reply_kernel, half, capacity),
        name="reply",
        out_shape=shape((half * strides[0], 2 * width), BF16),
        in_specs=[SMEM] + [VMEM] * 6,
        out_specs=VMEM,
        compiler_params=params(16),
    )(asked, k, v, mirror_k, mirror_v, glob_here, glob_there)
    reply, low, high = lax.optimization_barrier((reply, low, high))
    arrived = swap(reply)

    block = (3 + RAND) * BLK + glob
    dk_out, dv_out, inner_k, inner_v, edge_low, edge_high, attention_rows, grad_queries = pl.pallas_call(
        functools.partial(attend_kernel, half, capacity),
        name="attend",
        out_shape=(
            shape((half * strides[2], width), BF16),
            shape((half * strides[1], width), BF16),
            shape((tokens, width), F32),
            shape((tokens, width), F32),
            shape((BLK, 2 * width), BF16),
            shape((BLK, 2 * width), BF16),
            shape((tokens, width), BF16),
            shape((tokens, width), BF16),
        ),
        in_specs=[SMEM] + [VMEM] * 8,
        out_specs=(VMEM,) * 8,
        scratch_shapes=[
            pltpu.VMEM((tokens + 2 * BLK, 2 * width), BF16),
            pltpu.VMEM((block, width), BF16),
            pltpu.VMEM((block, width), BF16),
            pltpu.VMEM((tokens + 2 * BLK, 2 * width), F32),
            pltpu.VMEM((glob, wide), F32),
        ],
        compiler_params=params(32),
    )(places, q, grad_attn, og, k, v, low, high, arrived)

    from_high = lax.ppermute(edge_low, "ctx", backward)
    from_low = lax.ppermute(edge_high, "ctx", forward)
    dv_back = swap(dv_out)
    dk_out, dv_back = lax.optimization_barrier((dk_out, dv_back))
    dk_back = swap(dk_out)

    def fold(name, back, inner, more):
        return pl.pallas_call(
            functools.partial(fold_kernel, half, capacity),
            name=name,
            out_shape=(shape((tokens, width), F32), shape((tokens, width), BF16)) + more,
            in_specs=[SMEM, VMEM, VMEM],
            out_specs=(VMEM,) * (2 + len(more)),
            scratch_shapes=[pltpu.VMEM((tokens, width), F32)],
            compiler_params=params(16),
        )(asked, back, inner)

    own_v, give_v, share = fold("fold_values", dv_back, inner_v, (shape((rows, wide), BF16),))
    weight_share = share[:, 2 * width :]
    glob_sum = share[:, : 2 * width].astype(F32) + lax.ppermute(
        share[:, : 2 * width], "ctx", mirror
    ).astype(F32)
    weight_sum = weight_share.astype(F32) + lax.ppermute(weight_share, "ctx", mirror).astype(F32)
    for step in range(1, batch):
        same, crossed = (
            lax.ppermute(
                weight_share,
                ("ctx", "batch"),
                [
                    (i * batch + b, (i + shift) % span * batch + (b + step) % batch)
                    for i in range(span)
                    for b in range(batch)
                ],
            ).astype(F32)
            for shift in (0, half)
        )
        weight_sum += same + crossed
    far_v = lax.ppermute(give_v, "ctx", mirror)
    dk_back, far_v = lax.optimization_barrier((dk_back, far_v))
    own_k, give_k = fold("fold_keys", dk_back, inner_k, ())
    far_k = lax.ppermute(give_k, "ctx", mirror)
    share = jnp.concatenate([glob_sum, weight_sum], axis=1).astype(BF16)
    share, own_k = lax.optimization_barrier((share, own_k))
    totals = swap(jnp.tile(share, (half, 1)))
    grad_weight = totals[:, 2 * width :].astype(F32)
    attended = dot(attention_rows, output_weight, 1, 0).astype(BF16)

    grad_keys, grad_values = pl.pallas_call(
        finish_kernel,
        name="finish",
        out_shape=(shape((tokens, width), BF16), shape((tokens, width), BF16)),
        in_specs=[SMEM] + [VMEM] * 8,
        out_specs=(VMEM,) * 2,
        scratch_shapes=[pltpu.VMEM((tokens, width), F32)],
        compiler_params=params(24),
    )(here, glob_pos, own_k, own_v, far_k, far_v, from_low, from_high, totals)
    return (
        attended[None],
        grad_queries[None],
        grad_keys[None],
        grad_values[None],
        grad_weight,
    )


def solution(mesh):
    in_specs = (
        P("batch", "ctx", None),
        P("batch", "ctx", None),
        P("batch", "ctx", None),
        P(),
        P("batch", "ctx", None),
        P("batch", "ctx", None),
        P("batch", None),
    )
    out_specs = (
        P("batch", "ctx", None),
        P("batch", "ctx", None),
        P("batch", "ctx", None),
        P("batch", "ctx", None),
        P(),
    )
    return jax.shard_map(shards, mesh=mesh, in_specs=in_specs, out_specs=out_specs, check_vma=False)
```

```python
import functools

import jax
import jax.numpy as jnp
from jax import lax
from jax.experimental import pallas as pl
from jax.experimental.pallas import tpu as pltpu
from jax.sharding import PartitionSpec as P

BLK = 64
HEADS = 4
RAND = 3
LANES = 128
MIB = 1024 * 1024
LOG2E = 1.4426950408889634

F32 = jnp.float32
BF16 = jnp.bfloat16
VMEM = pl.BlockSpec(memory_space=pltpu.VMEM)
SMEM = pl.BlockSpec(memory_space=pltpu.SMEM)


def params(mib):
    return pltpu.CompilerParams(vmem_limit_bytes=mib * MIB)


def dot(left, right, over_left, over_right):
    return lax.dot_general(
        left, right, (((over_left,), (over_right,)), ((), ())), preferred_element_type=F32
    )


def ask_kernel(half, capacity, strides, here_ref, want_ref, pos_ref, k_ref, v_ref,
               send_ref, place_ref, v_out_ref, count_ref, list_ref):
    tokens, width = k_ref.shape
    glob = pos_ref.shape[1]
    query_blocks = tokens // BLK
    requests = query_blocks * RAND
    rows = glob // half
    lists = 2 * capacity
    me = here_ref[0]
    my_half = lax.div(me, half)
    for entry in range(2 * half):
        count_ref[entry] = 0
    for entry in range(half * lists):
        list_ref[entry] = -1

    def request(at, carry):
        wanted = want_ref[at]
        owner = lax.div(wanted, query_blocks)
        rank = jnp.minimum(count_ref[owner], capacity - 1)
        count_ref[owner] = count_ref[owner] + 1
        owner_half = lax.div(owner, half)
        member = owner - owner_half * half
        slot = jnp.where(owner_half == my_half, 0, capacity) + rank
        list_ref[member * lists + slot] = wanted - owner * query_blocks
        for use in range(3):
            place_ref[use * requests + at] = member * strides[use] + slot * BLK
        return carry

    lax.fori_loop(0, requests, request, 0)
    here = me * tokens + lax.broadcasted_iota(jnp.int32, (tokens, glob), 0)
    owned = jnp.where(here == pos_ref[...], 1.0, 0.0).astype(BF16)
    send_ref[:, :width] = dot(owned, k_ref[...], 0, 0).astype(BF16)
    send_ref[:, width : 2 * width] = dot(owned, v_ref[...], 0, 0).astype(BF16)
    v_out_ref[...] = v_ref[...]
    lane = lax.broadcasted_iota(jnp.int32, (rows, LANES), 1)
    for member in range(half):
        listed = jnp.full((rows, LANES), -1, jnp.int32)
        for slot in range(lists):
            listed = jnp.where(lane == slot, list_ref[member * lists + slot], listed)
        send_ref[member * rows : (member + 1) * rows, 2 * width :] = listed.astype(F32).astype(BF16)


def heard_kernel(half, got_ref, glob_ref, asked_ref):
    glob = got_ref.shape[0]
    rows = glob // half
    wide = glob_ref.shape[1]
    source = lax.broadcasted_iota(jnp.int32, (half, glob), 1)
    target = lax.broadcasted_iota(jnp.int32, (half, glob), 0)
    pick = jnp.where(source == target * rows, 1.0, 0.0).astype(BF16)
    asked_ref[...] = dot(pick, got_ref[:, wide:], 1, 0).astype(jnp.int32)
    source = lax.broadcasted_iota(jnp.int32, (rows, glob), 1)
    target = lax.broadcasted_iota(jnp.int32, (rows, glob), 0)
    total = jnp.where(lax.rem(source, rows) == target, 1.0, 0.0).astype(BF16)
    glob_ref[...] = dot(total, got_ref[:, :wide], 1, 0).astype(BF16)


def reply_kernel(half, capacity, asked_ref, k_ref, v_ref, mk_ref, mv_ref, glob_ref, mglob_ref, out_ref):
    tokens, width = k_ref.shape
    stride = out_ref.shape[0] // half
    share = (glob_ref[...].astype(F32) + mglob_ref[...].astype(F32)).astype(BF16)
    for member in range(half):
        for slot in range(2 * capacity):
            block = jnp.maximum(asked_ref[member, slot], 0)
            source = pl.ds(pl.multiple_of(block * BLK, BLK), BLK)
            target = pl.ds(member * stride + slot * BLK, BLK)
            own = slot < capacity
            out_ref[target, :width] = (k_ref if own else mk_ref)[source, :]
            out_ref[target, width:] = (v_ref if own else mv_ref)[source, :]
        out_ref[member * stride + 2 * capacity * BLK : (member + 1) * stride, :] = share


def attend_kernel(half, capacity, place_ref, q_ref, ga_ref, og_ref, k_ref, v_ref, low_ref, high_ref, arr_ref,
                  dk_out_ref, dv_out_ref, inner_k_ref, inner_v_ref, elow_ref, ehigh_ref, att_ref, dq_ref,
                  pad_ref, kc_ref, vc_ref, acc_ref, gacc_ref):
    tokens, width = q_ref.shape
    query_blocks = tokens // BLK
    head_size = width // HEADS
    scale = head_size ** (-0.5)
    win, local = 3 * BLK, (3 + RAND) * BLK
    requests = query_blocks * RAND
    pad_ref[:BLK] = low_ref[...]
    pad_ref[BLK : BLK + tokens, :width] = k_ref[...]
    pad_ref[BLK : BLK + tokens, width:] = v_ref[...]
    pad_ref[BLK + tokens :] = high_ref[...]
    skip = 2 * capacity * BLK
    rows = gacc_ref.shape[0] // half
    for member in range(half):
        at = member * (arr_ref.shape[0] // half) + skip
        kc_ref[local + member * rows : local + (member + 1) * rows] = arr_ref[at : at + rows, :width]
        vc_ref[local + member * rows : local + (member + 1) * rows] = arr_ref[at : at + rows, width:]
    acc_ref[...] = jnp.zeros_like(acc_ref)
    gacc_ref[...] = jnp.zeros_like(gacc_ref)
    row_head = lax.broadcasted_iota(jnp.int32, (HEADS * BLK, width), 0) // BLK
    lane_head = lax.broadcasted_iota(jnp.int32, (HEADS * BLK, width), 1) // head_size
    mask = jnp.where(row_head == lane_head, 1.0, 0.0).astype(BF16)
    keep = jnp.where(row_head == lane_head, 1.0, 0.0)

    def by_head(rows):
        return jnp.concatenate([rows] * HEADS, axis=0) * mask

    def own_head(full):
        kept = full * keep
        return sum(kept[h * BLK : (h + 1) * BLK] for h in range(HEADS))

    def one_block(i, carry):
        base = pl.multiple_of(i * BLK, BLK)
        kc_ref[:win] = pad_ref[pl.ds(base, win), :width]
        vc_ref[:win] = pad_ref[pl.ds(base, win), width:]
        for j in range(RAND):
            slot = pl.ds(pl.multiple_of(place_ref[i * RAND + j], BLK), BLK)
            kc_ref[win + j * BLK : win + (j + 1) * BLK] = arr_ref[slot, :width]
            vc_ref[win + j * BLK : win + (j + 1) * BLK] = arr_ref[slot, width:]
        q_by_head = by_head(q_ref[pl.ds(base, BLK), :])
        ga_by_head = by_head(ga_ref[pl.ds(base, BLK), :])
        scores = dot(kc_ref[...], q_by_head, 1, 1) * (scale * LOG2E)
        expo = jnp.exp2(scores - jnp.max(scores, axis=0, keepdims=True))
        probs = expo * (1.0 / jnp.sum(expo, axis=0, keepdims=True))
        probs16 = probs.astype(BF16)
        dprobs = dot(vc_ref[...], ga_by_head, 1, 1)
        delta = jnp.sum(probs16.astype(F32) * dprobs, axis=0, keepdims=True)
        dscores = (probs * (dprobs - delta) * scale).astype(BF16)
        att_ref[pl.ds(base, BLK), :] = own_head(dot(probs16, vc_ref[...], 0, 0)).astype(BF16)
        dq_ref[pl.ds(base, BLK), :] = own_head(dot(dscores, kc_ref[...], 0, 0)).astype(BF16)
        for out_ref, at, part, terms in (
            (dv_out_ref, 1, slice(width, 2 * width), dot(probs16, ga_by_head, 1, 0)),
            (dk_out_ref, 2, slice(0, width), dot(dscores, q_by_head, 1, 0)),
        ):
            acc_ref[pl.ds(base, win), part] += terms[:win]
            gacc_ref[:, part] += terms[local:]
            for j in range(RAND):
                slot = place_ref[at * requests + i * RAND + j]
                out_ref[pl.ds(pl.multiple_of(slot, 16), BLK), :] = terms[
                    win + j * BLK : win + (j + 1) * BLK
                ].astype(BF16)
        return carry

    lax.fori_loop(0, query_blocks, one_block, 0, unroll=4)
    inner_k_ref[...] = acc_ref[BLK : BLK + tokens, :width]
    inner_v_ref[...] = acc_ref[BLK : BLK + tokens, width:]
    elow_ref[...] = acc_ref[:BLK].astype(BF16)
    ehigh_ref[...] = acc_ref[BLK + tokens :].astype(BF16)
    gacc_ref[:, 2 * width :] = dot(att_ref[...], og_ref[...], 0, 0)
    stride = dv_out_ref.shape[0] // half
    for member in range(half):
        for part in range(gacc_ref.shape[1] // width):
            at = member * stride + skip + part * rows
            dv_out_ref[at : at + rows, :] = gacc_ref[
                member * rows : (member + 1) * rows, part * width : (part + 1) * width
            ].astype(BF16)


def fold_kernel(half, capacity, asked_ref, back_ref, inner_ref, own_ref, give_ref, mirror_acc):
    tokens = own_ref.shape[0]
    stride = back_ref.shape[0] // half
    skip = 2 * capacity * BLK
    own_ref[...] = inner_ref[...]
    mirror_acc[...] = jnp.zeros_like(mirror_acc)
    for member in range(half):
        for slot in range(2 * capacity):
            block = asked_ref[member, slot]
            acc_ref = own_ref if slot < capacity else mirror_acc
            at = member * stride + slot * BLK

            @pl.when(block >= 0)
            def _():
                rows = pl.ds(pl.multiple_of(block * BLK, BLK), BLK)
                acc_ref[rows, :] += back_ref[at : at + BLK, :].astype(F32)

    give_ref[:tokens] = mirror_acc[...].astype(BF16)
    if stride > skip:
        total = back_ref[skip:stride, :].astype(F32)
        for member in range(1, half):
            total += back_ref[member * stride + skip : (member + 1) * stride, :].astype(F32)
        give_ref[tokens:] = total.astype(BF16)


def finish_kernel(half, here_ref, pos_ref, own_k_ref, own_v_ref, far_k_ref, far_v_ref, from_low_ref,
                  from_high_ref, total_ref, dk_ref, dv_ref, weight_ref, acc_ref, glob_ref):
    tokens, width = dk_ref.shape
    glob = pos_ref.shape[1]
    rows = glob // half
    stride = total_ref.shape[0] // half
    here = here_ref[0] * tokens + lax.broadcasted_iota(jnp.int32, (tokens, glob), 0)
    owned = jnp.where(here == pos_ref[...], 1.0, 0.0).astype(BF16)
    for member in range(half):
        mine = slice(member * rows, (member + 1) * rows)
        for part in range(stride // rows):
            at = member * stride + part * rows
            if part < 2:
                glob_ref[mine, part * width : (part + 1) * width] = total_ref[at : at + rows, :]
            else:
                weight_ref[mine, (part - 2) * width : (part - 1) * width] = total_ref[
                    at : at + rows, :
                ].astype(F32)
    for part, own_ref, far_ref, out_ref in (
        (slice(0, width), own_k_ref, far_k_ref, dk_ref),
        (slice(width, 2 * width), own_v_ref, far_v_ref, dv_ref),
    ):
        acc_ref[...] = own_ref[...] + far_ref[:tokens].astype(F32) + dot(owned, glob_ref[:, part], 1, 0)
        acc_ref[:BLK] += from_low_ref[:, part].astype(F32)
        acc_ref[tokens - BLK :] += from_high_ref[:, part].astype(F32)
        out_ref[...] = acc_ref[...].astype(BF16)


def shards(queries, keys, values, output_weight, output_grad, rand_blocks, glob_pos):
    q, k, v, og = queries[0], keys[0], values[0], output_grad[0]
    tokens, width = q.shape
    model = og.shape[1]
    glob = glob_pos.shape[1]
    query_blocks = tokens // BLK
    span = lax.axis_size("ctx")
    batch = lax.axis_size("batch")
    requests = query_blocks * RAND
    capacity = requests // span + 1
    half = span // 2
    rows = glob // half
    wide = 2 * width + model
    skip = 2 * capacity * BLK
    strides = (skip + rows, skip + rows * wide // width, skip)
    here = lax.axis_index("ctx").astype(jnp.int32).reshape(1)
    shape = jax.ShapeDtypeStruct
    forward = [(i, (i + 1) % span) for i in range(span)]
    backward = [(target, source) for source, target in forward]
    mirror = [(i, (i + half) % span) for i in range(span)]
    halves = [list(range(half)), list(range(half, span))]

    def swap(x):
        return lax.all_to_all(
            x, "ctx", split_axis=0, concat_axis=0, axis_index_groups=halves, tiled=True
        )

    mirror_k = lax.ppermute(k, "ctx", mirror)
    send, places, v_after = pl.pallas_call(
        functools.partial(ask_kernel, half, capacity, strides),
        name="ask",
        out_shape=(
            shape((glob, 2 * width + LANES), BF16),
            shape((3 * requests,), jnp.int32),
            shape((tokens, width), BF16),
        ),
        in_specs=[SMEM, SMEM, VMEM, VMEM, VMEM],
        out_specs=(VMEM, SMEM, VMEM),
        scratch_shapes=[pltpu.SMEM((span,), jnp.int32), pltpu.SMEM((span * capacity,), jnp.int32)],
        compiler_params=params(60),
    )(here, rand_blocks.reshape(requests), glob_pos, k, v)
    got = swap(send)
    mirror_v = lax.ppermute(v_after, "ctx", mirror)
    key_value_edges = [
        jnp.concatenate([k[edge], v[edge]], axis=1)
        for edge in (slice(tokens - BLK, tokens), slice(0, BLK))
    ]
    low = lax.ppermute(key_value_edges[0], "ctx", forward)
    high = lax.ppermute(key_value_edges[1], "ctx", backward)
    grad_attn = dot(og, output_weight, 1, 1).astype(BF16)

    glob_here, asked = pl.pallas_call(
        functools.partial(heard_kernel, half),
        name="heard",
        out_shape=(shape((rows, 2 * width), BF16), shape((half, LANES), jnp.int32)),
        in_specs=[VMEM],
        out_specs=(VMEM,) * 2,
        compiler_params=params(16),
    )(got)
    glob_there = lax.ppermute(glob_here, "ctx", mirror)
    reply = pl.pallas_call(
        functools.partial(reply_kernel, half, capacity),
        name="reply",
        out_shape=shape((half * strides[0], 2 * width), BF16),
        in_specs=[SMEM] + [VMEM] * 6,
        out_specs=VMEM,
        compiler_params=params(60),
    )(asked, k, v, mirror_k, mirror_v, glob_here, glob_there)
    reply, low, high = lax.optimization_barrier((reply, low, high))
    arrived = swap(reply)

    block = (3 + RAND) * BLK + glob
    dk_out, dv_out, inner_k, inner_v, edge_low, edge_high, attention_rows, grad_queries = pl.pallas_call(
        functools.partial(attend_kernel, half, capacity),
        name="attend",
        out_shape=(
            shape((half * strides[2], width), BF16),
            shape((half * strides[1], width), BF16),
            shape((tokens, width), F32),
            shape((tokens, width), F32),
            shape((BLK, 2 * width), BF16),
            shape((BLK, 2 * width), BF16),
            shape((tokens, width), BF16),
            shape((tokens, width), BF16),
        ),
        in_specs=[SMEM] + [VMEM] * 8,
        out_specs=(VMEM,) * 8,
        scratch_shapes=[
            pltpu.VMEM((tokens + 2 * BLK, 2 * width), BF16),
            pltpu.VMEM((block, width), BF16),
            pltpu.VMEM((block, width), BF16),
            pltpu.VMEM((tokens + 2 * BLK, 2 * width), F32),
            pltpu.VMEM((glob, wide), F32),
        ],
        compiler_params=params(32),
    )(places, q, grad_attn, og, k, v, low, high, arrived)

    from_high = lax.ppermute(edge_low, "ctx", backward)
    from_low = lax.ppermute(edge_high, "ctx", forward)
    dv_back = swap(dv_out)
    dk_out, dv_back = lax.optimization_barrier((dk_out, dv_back))
    dk_back = swap(dk_out)

    def fold(name, back, inner, more):
        return pl.pallas_call(
            functools.partial(fold_kernel, half, capacity),
            name=name,
            out_shape=(shape((tokens, width), F32), shape((tokens + more, width), BF16)),
            in_specs=[SMEM, VMEM, VMEM],
            out_specs=(VMEM,) * 2,
            scratch_shapes=[pltpu.VMEM((tokens, width), F32)],
            compiler_params=params(16),
        )(asked, back, inner)

    own_v, give_v = fold("fold_values", dv_back, inner_v, strides[1] - skip)
    far_v = lax.ppermute(give_v, "ctx", mirror)
    far_v, from_high, from_low = lax.optimization_barrier((far_v, from_high, from_low))
    weight_at = tokens + 2 * rows
    weight_share = give_v[weight_at:]
    weight_sum = weight_share.astype(F32) + far_v[weight_at:].astype(F32)
    for step in range(1, batch):
        same, crossed = (
            lax.ppermute(
                weight_share,
                ("ctx", "batch"),
                [
                    (i * batch + b, (i + shift) % span * batch + (b + step) % batch)
                    for i in range(span)
                    for b in range(batch)
                ],
            ).astype(F32)
            for shift in (0, half)
        )
        weight_sum += same + crossed
    glob_sum = give_v[tokens:weight_at].astype(F32) + far_v[tokens:weight_at].astype(F32)
    share = jnp.concatenate([glob_sum, weight_sum], axis=0).astype(BF16)
    own_k, give_k = fold("fold_keys", dk_back, inner_k, 0)
    far_k = lax.ppermute(give_k, "ctx", mirror)
    share, own_k = lax.optimization_barrier((share, own_k))
    totals = swap(jnp.tile(share, (half, 1)))
    attended = dot(attention_rows, output_weight, 1, 0).astype(BF16)

    grad_keys, grad_values, grad_weight = pl.pallas_call(
        functools.partial(finish_kernel, half),
        name="finish",
        out_shape=(
            shape((tokens, width), BF16),
            shape((tokens, width), BF16),
            shape((width, model), F32),
        ),
        in_specs=[SMEM] + [VMEM] * 8,
        out_specs=(VMEM,) * 3,
        scratch_shapes=[
            pltpu.VMEM((tokens, width), F32),
            pltpu.VMEM((glob, 2 * width), BF16),
        ],
        compiler_params=params(24),
    )(here, glob_pos, own_k, own_v, far_k, far_v, from_low, from_high, totals)
    return (
        attended[None],
        grad_queries[None],
        grad_keys[None],
        grad_values[None],
        grad_weight,
    )


def solution(mesh):
    in_specs = (
        P("batch", "ctx", None),
        P("batch", "ctx", None),
        P("batch", "ctx", None),
        P(),
        P("batch", "ctx", None),
        P("batch", "ctx", None),
        P("batch", None),
    )
    out_specs = (
        P("batch", "ctx", None),
        P("batch", "ctx", None),
        P("batch", "ctx", None),
        P("batch", "ctx", None),
        P(),
    )
    return jax.shard_map(shards, mesh=mesh, in_specs=in_specs, out_specs=out_specs, check_vma=False)
```

```python
import functools

import jax
import jax.numpy as jnp
from jax import lax
from jax.experimental import pallas as pl
from jax.experimental.pallas import tpu as pltpu
from jax.sharding import PartitionSpec as P

BLK = 64
HEADS = 4
RAND = 3
LANES = 128
MIB = 1024 * 1024
LOG2E = 1.4426950408889634

F32 = jnp.float32
BF16 = jnp.bfloat16
VMEM = pl.BlockSpec(memory_space=pltpu.VMEM)
SMEM = pl.BlockSpec(memory_space=pltpu.SMEM)


def params(mib):
    return pltpu.CompilerParams(vmem_limit_bytes=mib * MIB)


def dot(left, right, over_left, over_right):
    return lax.dot_general(
        left, right, (((over_left,), (over_right,)), ((), ())), preferred_element_type=F32
    )


def ask_kernel(half, capacity, strides, here_ref, want_ref, pos_ref, k_ref, v_ref,
               send_ref, place_ref, v_out_ref, count_ref, list_ref):
    tokens, width = k_ref.shape
    glob = pos_ref.shape[1]
    query_blocks = tokens // BLK
    requests = query_blocks * RAND
    rows = glob // half
    lists = 2 * capacity
    me = here_ref[0]
    my_half = lax.div(me, half)
    for entry in range(2 * half):
        count_ref[entry] = 0
    for entry in range(half * lists):
        list_ref[entry] = -1

    def request(at, carry):
        wanted = want_ref[at]
        owner = lax.div(wanted, query_blocks)
        rank = jnp.minimum(count_ref[owner], capacity - 1)
        count_ref[owner] = count_ref[owner] + 1
        owner_half = lax.div(owner, half)
        member = owner - owner_half * half
        slot = jnp.where(owner_half == my_half, 0, capacity) + rank
        list_ref[member * lists + slot] = wanted - owner * query_blocks
        for use in range(3):
            place_ref[use * requests + at] = member * strides[use] + slot * BLK
        return carry

    lax.fori_loop(0, requests, request, 0)
    here = me * tokens + lax.broadcasted_iota(jnp.int32, (tokens, glob), 0)
    owned = jnp.where(here == pos_ref[...], 1.0, 0.0).astype(BF16)
    send_ref[:, :width] = dot(owned, k_ref[...], 0, 0).astype(BF16)
    send_ref[:, width : 2 * width] = dot(owned, v_ref[...], 0, 0).astype(BF16)
    v_out_ref[...] = v_ref[...]
    lane = lax.broadcasted_iota(jnp.int32, (rows, LANES), 1)
    for member in range(half):
        listed = jnp.full((rows, LANES), -1, jnp.int32)
        for slot in range(lists):
            listed = jnp.where(lane == slot, list_ref[member * lists + slot], listed)
        send_ref[member * rows : (member + 1) * rows, 2 * width :] = listed.astype(F32).astype(BF16)


def heard_kernel(half, got_ref, glob_ref, asked_ref):
    glob = got_ref.shape[0]
    rows = glob // half
    wide = glob_ref.shape[1]
    source = lax.broadcasted_iota(jnp.int32, (half, glob), 1)
    target = lax.broadcasted_iota(jnp.int32, (half, glob), 0)
    pick = jnp.where(source == target * rows, 1.0, 0.0).astype(BF16)
    asked_ref[...] = dot(pick, got_ref[:, wide:], 1, 0).astype(jnp.int32)
    source = lax.broadcasted_iota(jnp.int32, (rows, glob), 1)
    target = lax.broadcasted_iota(jnp.int32, (rows, glob), 0)
    total = jnp.where(lax.rem(source, rows) == target, 1.0, 0.0).astype(BF16)
    glob_ref[...] = dot(total, got_ref[:, :wide], 1, 0).astype(BF16)


def reply_kernel(half, capacity, asked_ref, k_ref, v_ref, mk_ref, mv_ref, glob_ref, mglob_ref, out_ref):
    tokens, width = k_ref.shape
    stride = out_ref.shape[0] // half
    share = (glob_ref[...].astype(F32) + mglob_ref[...].astype(F32)).astype(BF16)
    for member in range(half):
        for slot in range(2 * capacity):
            block = jnp.maximum(asked_ref[member, slot], 0)
            source = pl.ds(pl.multiple_of(block * BLK, BLK), BLK)
            target = pl.ds(member * stride + slot * BLK, BLK)
            own = slot < capacity
            out_ref[target, :width] = (k_ref if own else mk_ref)[source, :]
            out_ref[target, width:] = (v_ref if own else mv_ref)[source, :]
        out_ref[member * stride + 2 * capacity * BLK : (member + 1) * stride, :] = share


def attend_kernel(half, capacity, place_ref, q_ref, ga_ref, og_ref, k_ref, v_ref, low_ref, high_ref, arr_ref,
                  dk_out_ref, dv_out_ref, inner_k_ref, inner_v_ref, elow_ref, ehigh_ref, att_ref, dq_ref,
                  pad_ref, kc_ref, vc_ref, acc_ref, gacc_ref):
    tokens, width = q_ref.shape
    query_blocks = tokens // BLK
    head_size = width // HEADS
    scale = head_size ** (-0.5)
    win, local = 3 * BLK, (3 + RAND) * BLK
    requests = query_blocks * RAND
    pad_ref[:BLK] = low_ref[...]
    pad_ref[BLK : BLK + tokens, :width] = k_ref[...]
    pad_ref[BLK : BLK + tokens, width:] = v_ref[...]
    pad_ref[BLK + tokens :] = high_ref[...]
    skip = 2 * capacity * BLK
    rows = gacc_ref.shape[0] // half
    for member in range(half):
        at = member * (arr_ref.shape[0] // half) + skip
        kc_ref[local + member * rows : local + (member + 1) * rows] = arr_ref[at : at + rows, :width]
        vc_ref[local + member * rows : local + (member + 1) * rows] = arr_ref[at : at + rows, width:]
    acc_ref[...] = jnp.zeros_like(acc_ref)
    gacc_ref[...] = jnp.zeros_like(gacc_ref)
    row_head = lax.broadcasted_iota(jnp.int32, (HEADS * BLK, width), 0) // BLK
    lane_head = lax.broadcasted_iota(jnp.int32, (HEADS * BLK, width), 1) // head_size
    mask = jnp.where(row_head == lane_head, 1.0, 0.0).astype(BF16)
    keep = jnp.where(row_head == lane_head, 1.0, 0.0)

    def by_head(rows):
        return jnp.concatenate([rows] * HEADS, axis=0) * mask

    def own_head(full):
        kept = full * keep
        return sum(kept[h * BLK : (h + 1) * BLK] for h in range(HEADS))

    def one_block(i, carry):
        base = pl.multiple_of(i * BLK, BLK)
        kc_ref[:win] = pad_ref[pl.ds(base, win), :width]
        vc_ref[:win] = pad_ref[pl.ds(base, win), width:]
        for j in range(RAND):
            slot = pl.ds(pl.multiple_of(place_ref[i * RAND + j], BLK), BLK)
            kc_ref[win + j * BLK : win + (j + 1) * BLK] = arr_ref[slot, :width]
            vc_ref[win + j * BLK : win + (j + 1) * BLK] = arr_ref[slot, width:]
        q_by_head = by_head(q_ref[pl.ds(base, BLK), :])
        ga_by_head = by_head(ga_ref[pl.ds(base, BLK), :])
        scores = dot(kc_ref[...], q_by_head, 1, 1) * (scale * LOG2E)
        expo = jnp.exp2(scores - jnp.max(scores, axis=0, keepdims=True))
        probs = expo * (1.0 / jnp.sum(expo, axis=0, keepdims=True))
        probs16 = probs.astype(BF16)
        dprobs = dot(vc_ref[...], ga_by_head, 1, 1)
        delta = jnp.sum(probs16.astype(F32) * dprobs, axis=0, keepdims=True)
        dscores = (probs * (dprobs - delta) * scale).astype(BF16)
        att_ref[pl.ds(base, BLK), :] = own_head(dot(probs16, vc_ref[...], 0, 0)).astype(BF16)
        dq_ref[pl.ds(base, BLK), :] = own_head(dot(dscores, kc_ref[...], 0, 0)).astype(BF16)
        for out_ref, at, part, terms in (
            (dv_out_ref, 1, slice(width, 2 * width), dot(probs16, ga_by_head, 1, 0)),
            (dk_out_ref, 2, slice(0, width), dot(dscores, q_by_head, 1, 0)),
        ):
            acc_ref[pl.ds(base, win), part] += terms[:win]
            gacc_ref[:, part] += terms[local:]
            for j in range(RAND):
                slot = place_ref[at * requests + i * RAND + j]
                out_ref[pl.ds(pl.multiple_of(slot, 16), BLK), :] = terms[
                    win + j * BLK : win + (j + 1) * BLK
                ].astype(BF16)
        return carry

    lax.fori_loop(0, query_blocks, one_block, 0, unroll=8)
    inner_k_ref[...] = acc_ref[BLK : BLK + tokens, :width]
    inner_v_ref[...] = acc_ref[BLK : BLK + tokens, width:]
    elow_ref[...] = acc_ref[:BLK].astype(BF16)
    ehigh_ref[...] = acc_ref[BLK + tokens :].astype(BF16)
    gacc_ref[:, 2 * width :] = dot(att_ref[...], og_ref[...], 0, 0)
    stride = dv_out_ref.shape[0] // half
    for member in range(half):
        for part in range(gacc_ref.shape[1] // width):
            at = member * stride + skip + part * rows
            dv_out_ref[at : at + rows, :] = gacc_ref[
                member * rows : (member + 1) * rows, part * width : (part + 1) * width
            ].astype(BF16)


def fold_kernel(half, capacity, asked_ref, back_ref, inner_ref, own_ref, give_ref, mirror_acc):
    tokens = own_ref.shape[0]
    stride = back_ref.shape[0] // half
    skip = 2 * capacity * BLK
    own_ref[...] = inner_ref[...]
    mirror_acc[...] = jnp.zeros_like(mirror_acc)
    for member in range(half):
        for slot in range(2 * capacity):
            block = asked_ref[member, slot]
            acc_ref = own_ref if slot < capacity else mirror_acc
            at = member * stride + slot * BLK

            @pl.when(block >= 0)
            def _():
                rows = pl.ds(pl.multiple_of(block * BLK, BLK), BLK)
                acc_ref[rows, :] += back_ref[at : at + BLK, :].astype(F32)

    give_ref[:tokens] = mirror_acc[...].astype(BF16)
    if stride > skip:
        total = back_ref[skip:stride, :].astype(F32)
        for member in range(1, half):
            total += back_ref[member * stride + skip : (member + 1) * stride, :].astype(F32)
        give_ref[tokens:] = total.astype(BF16)


def finish_kernel(half, here_ref, pos_ref, own_k_ref, own_v_ref, far_k_ref, far_v_ref, from_low_ref,
                  from_high_ref, total_ref, dk_ref, dv_ref, weight_ref, acc_ref, glob_ref):
    tokens, width = dk_ref.shape
    glob = pos_ref.shape[1]
    rows = glob // half
    stride = total_ref.shape[0] // half
    here = here_ref[0] * tokens + lax.broadcasted_iota(jnp.int32, (tokens, glob), 0)
    owned = jnp.where(here == pos_ref[...], 1.0, 0.0).astype(BF16)
    for member in range(half):
        mine = slice(member * rows, (member + 1) * rows)
        for part in range(stride // rows):
            at = member * stride + part * rows
            if part < 2:
                glob_ref[mine, part * width : (part + 1) * width] = total_ref[at : at + rows, :]
            else:
                weight_ref[mine, (part - 2) * width : (part - 1) * width] = total_ref[
                    at : at + rows, :
                ].astype(F32)
    for part, own_ref, far_ref, out_ref in (
        (slice(0, width), own_k_ref, far_k_ref, dk_ref),
        (slice(width, 2 * width), own_v_ref, far_v_ref, dv_ref),
    ):
        acc_ref[...] = own_ref[...] + far_ref[:tokens].astype(F32) + dot(owned, glob_ref[:, part], 1, 0)
        acc_ref[:BLK] += from_low_ref[:, part].astype(F32)
        acc_ref[tokens - BLK :] += from_high_ref[:, part].astype(F32)
        out_ref[...] = acc_ref[...].astype(BF16)


def shards(queries, keys, values, output_weight, output_grad, rand_blocks, glob_pos):
    q, k, v, og = queries[0], keys[0], values[0], output_grad[0]
    tokens, width = q.shape
    model = og.shape[1]
    glob = glob_pos.shape[1]
    query_blocks = tokens // BLK
    span = lax.axis_size("ctx")
    batch = lax.axis_size("batch")
    requests = query_blocks * RAND
    capacity = requests // span + 1
    half = span // 2
    rows = glob // half
    wide = 2 * width + model
    skip = 2 * capacity * BLK
    strides = (skip + rows, skip + rows * wide // width, skip)
    here = lax.axis_index("ctx").astype(jnp.int32).reshape(1)
    shape = jax.ShapeDtypeStruct
    forward = [(i, (i + 1) % span) for i in range(span)]
    backward = [(target, source) for source, target in forward]
    mirror = [(i, (i + half) % span) for i in range(span)]
    halves = [list(range(half)), list(range(half, span))]

    def swap(x):
        return lax.all_to_all(
            x, "ctx", split_axis=0, concat_axis=0, axis_index_groups=halves, tiled=True
        )

    mirror_k = lax.ppermute(k, "ctx", mirror)
    send, places, v_after = pl.pallas_call(
        functools.partial(ask_kernel, half, capacity, strides),
        name="ask",
        out_shape=(
            shape((glob, 2 * width + LANES), BF16),
            shape((3 * requests,), jnp.int32),
            shape((tokens, width), BF16),
        ),
        in_specs=[SMEM, SMEM, VMEM, VMEM, VMEM],
        out_specs=(VMEM, SMEM, VMEM),
        scratch_shapes=[pltpu.SMEM((span,), jnp.int32), pltpu.SMEM((span * capacity,), jnp.int32)],
        compiler_params=params(60),
    )(here, rand_blocks.reshape(requests), glob_pos, k, v)
    got = swap(send)
    mirror_v = lax.ppermute(v_after, "ctx", mirror)
    key_value_edges = [
        jnp.concatenate([k[edge], v[edge]], axis=1)
        for edge in (slice(tokens - BLK, tokens), slice(0, BLK))
    ]
    low = lax.ppermute(key_value_edges[0], "ctx", forward)
    high = lax.ppermute(key_value_edges[1], "ctx", backward)
    grad_attn = dot(og, output_weight, 1, 1).astype(BF16)

    glob_here, asked = pl.pallas_call(
        functools.partial(heard_kernel, half),
        name="heard",
        out_shape=(shape((rows, 2 * width), BF16), shape((half, LANES), jnp.int32)),
        in_specs=[VMEM],
        out_specs=(VMEM,) * 2,
        compiler_params=params(16),
    )(got)
    glob_there = lax.ppermute(glob_here, "ctx", mirror)
    reply = pl.pallas_call(
        functools.partial(reply_kernel, half, capacity),
        name="reply",
        out_shape=shape((half * strides[0], 2 * width), BF16),
        in_specs=[SMEM] + [VMEM] * 6,
        out_specs=VMEM,
        compiler_params=params(60),
    )(asked, k, v, mirror_k, mirror_v, glob_here, glob_there)
    reply, low, high = lax.optimization_barrier((reply, low, high))
    arrived = swap(reply)

    block = (3 + RAND) * BLK + glob
    dk_out, dv_out, inner_k, inner_v, edge_low, edge_high, attention_rows, grad_queries = pl.pallas_call(
        functools.partial(attend_kernel, half, capacity),
        name="attend",
        out_shape=(
            shape((half * strides[2], width), BF16),
            shape((half * strides[1], width), BF16),
            shape((tokens, width), F32),
            shape((tokens, width), F32),
            shape((BLK, 2 * width), BF16),
            shape((BLK, 2 * width), BF16),
            shape((tokens, width), BF16),
            shape((tokens, width), BF16),
        ),
        in_specs=[SMEM] + [VMEM] * 8,
        out_specs=(VMEM,) * 8,
        scratch_shapes=[
            pltpu.VMEM((tokens + 2 * BLK, 2 * width), BF16),
            pltpu.VMEM((block, width), BF16),
            pltpu.VMEM((block, width), BF16),
            pltpu.VMEM((tokens + 2 * BLK, 2 * width), F32),
            pltpu.VMEM((glob, wide), F32),
        ],
        compiler_params=params(32),
    )(places, q, grad_attn, og, k, v, low, high, arrived)

    from_high = lax.ppermute(edge_low, "ctx", backward)
    from_low = lax.ppermute(edge_high, "ctx", forward)
    dv_back = swap(dv_out)
    dk_out, dv_back = lax.optimization_barrier((dk_out, dv_back))
    dk_back = swap(dk_out)

    def fold(name, back, inner, more):
        return pl.pallas_call(
            functools.partial(fold_kernel, half, capacity),
            name=name,
            out_shape=(shape((tokens, width), F32), shape((tokens + more, width), BF16)),
            in_specs=[SMEM, VMEM, VMEM],
            out_specs=(VMEM,) * 2,
            scratch_shapes=[pltpu.VMEM((tokens, width), F32)],
            compiler_params=params(16),
        )(asked, back, inner)

    own_v, give_v = fold("fold_values", dv_back, inner_v, strides[1] - skip)
    far_v = lax.ppermute(give_v, "ctx", mirror)
    far_v, from_high, from_low = lax.optimization_barrier((far_v, from_high, from_low))
    weight_at = tokens + 2 * rows
    weight_share = give_v[weight_at:]
    weight_sum = weight_share.astype(F32) + far_v[weight_at:].astype(F32)
    for step in range(1, batch):
        same, crossed = (
            lax.ppermute(
                weight_share,
                ("ctx", "batch"),
                [
                    (i * batch + b, (i + shift) % span * batch + (b + step) % batch)
                    for i in range(span)
                    for b in range(batch)
                ],
            ).astype(F32)
            for shift in (0, half)
        )
        weight_sum += same + crossed
    glob_sum = give_v[tokens:weight_at].astype(F32) + far_v[tokens:weight_at].astype(F32)
    share = jnp.concatenate([glob_sum, weight_sum], axis=0).astype(BF16)
    own_k, give_k = fold("fold_keys", dk_back, inner_k, 0)
    far_k = lax.ppermute(give_k, "ctx", mirror)
    share, own_k = lax.optimization_barrier((share, own_k))
    totals = lax.all_gather(share, "ctx", axis=0, axis_index_groups=halves, tiled=True)
    attended = dot(attention_rows, output_weight, 1, 0).astype(BF16)

    grad_keys, grad_values, grad_weight = pl.pallas_call(
        functools.partial(finish_kernel, half),
        name="finish",
        out_shape=(
            shape((tokens, width), BF16),
            shape((tokens, width), BF16),
            shape((width, model), F32),
        ),
        in_specs=[SMEM] + [VMEM] * 8,
        out_specs=(VMEM,) * 3,
        scratch_shapes=[
            pltpu.VMEM((tokens, width), F32),
            pltpu.VMEM((glob, 2 * width), BF16),
        ],
        compiler_params=params(24),
    )(here, glob_pos, own_k, own_v, far_k, far_v, from_low, from_high, totals)
    return (
        attended[None],
        grad_queries[None],
        grad_keys[None],
        grad_values[None],
        grad_weight,
    )


def solution(mesh):
    in_specs = (
        P("batch", "ctx", None),
        P("batch", "ctx", None),
        P("batch", "ctx", None),
        P(),
        P("batch", "ctx", None),
        P("batch", "ctx", None),
        P("batch", None),
    )
    out_specs = (
        P("batch", "ctx", None),
        P("batch", "ctx", None),
        P("batch", "ctx", None),
        P("batch", "ctx", None),
        P(),
    )
    return jax.shard_map(shards, mesh=mesh, in_specs=in_specs, out_specs=out_specs, check_vma=False)
```

```python
import functools

import jax
import jax.numpy as jnp
from jax import lax
from jax.experimental import pallas as pl
from jax.experimental.pallas import tpu as pltpu
from jax.sharding import PartitionSpec as P

BLK = 64
HEADS = 4
RAND = 3
LANES = 128
MIB = 1024 * 1024
LOG2E = 1.4426950408889634
MASKS = (0, 6, 2, 4, 7, 3, 5, 1)

F32 = jnp.float32
BF16 = jnp.bfloat16
VMEM = pl.BlockSpec(memory_space=pltpu.VMEM)
SMEM = pl.BlockSpec(memory_space=pltpu.SMEM)


def params(mib):
    return pltpu.CompilerParams(vmem_limit_bytes=mib * MIB)


def dot(left, right, over_left, over_right):
    return lax.dot_general(
        left, right, (((over_left,), (over_right,)), ((), ())), preferred_element_type=F32
    )


def masks_of(half):
    return MASKS if half == len(MASKS) else tuple(range(half))


def member_of(here_ref, direct, half, j):
    return here_ref[1] ^ masks_of(half)[j] if direct else j


def rows_of(member, rows):
    if isinstance(member, int):
        return slice(member * rows, (member + 1) * rows)
    return pl.ds(pl.multiple_of(member * rows, rows), rows)


def ask_kernel(half, capacity, strides, here_ref, want_ref, pos_ref, k_ref, v_ref,
               send_ref, place_ref, v_out_ref, count_ref, list_ref):
    tokens, width = k_ref.shape
    glob = pos_ref.shape[1]
    query_blocks = tokens // BLK
    requests = query_blocks * RAND
    rows = glob // half
    lists = 2 * capacity
    me = here_ref[0]
    turn = here_ref[1]
    my_half = lax.div(me, half)
    for entry in range(2 * half):
        count_ref[entry] = 0
    for entry in range(half * lists):
        list_ref[entry] = -1

    def request(at, carry):
        wanted = want_ref[at]
        owner = lax.div(wanted, query_blocks)
        rank = jnp.minimum(count_ref[owner], capacity - 1)
        count_ref[owner] = count_ref[owner] + 1
        owner_half = lax.div(owner, half)
        member = owner - owner_half * half
        slot = jnp.where(owner_half == my_half, 0, capacity) + rank
        list_ref[member * lists + slot] = wanted - owner * query_blocks
        piece = member ^ turn
        piece = sum(jnp.where(piece == mask, j, 0) for j, mask in enumerate(masks_of(half)))
        for use, stride in enumerate(strides):
            place_ref[use * requests + at] = piece * stride + slot * BLK
        return carry

    lax.fori_loop(0, requests, request, 0)
    here = me * tokens + lax.broadcasted_iota(jnp.int32, (tokens, glob), 0)
    owned = jnp.where(here == pos_ref[...], 1.0, 0.0).astype(BF16)
    send_ref[:, :width] = dot(owned, k_ref[...], 0, 0).astype(BF16)
    send_ref[:, width : 2 * width] = dot(owned, v_ref[...], 0, 0).astype(BF16)
    v_out_ref[...] = v_ref[...]
    lane = lax.broadcasted_iota(jnp.int32, (rows, LANES), 1)
    for member in range(half):
        listed = jnp.full((rows, LANES), -1, jnp.int32)
        for slot in range(lists):
            listed = jnp.where(lane == slot, list_ref[member * lists + slot], listed)
        send_ref[member * rows : (member + 1) * rows, 2 * width :] = listed.astype(F32).astype(BF16)


def heard_kernel(half, got_ref, glob_ref, asked_ref):
    glob = got_ref.shape[0]
    rows = glob // half
    wide = glob_ref.shape[1]
    source = lax.broadcasted_iota(jnp.int32, (half, glob), 1)
    target = lax.broadcasted_iota(jnp.int32, (half, glob), 0)
    pick = jnp.where(source == target * rows, 1.0, 0.0).astype(BF16)
    asked_ref[...] = dot(pick, got_ref[:, wide:], 1, 0).astype(jnp.int32)
    source = lax.broadcasted_iota(jnp.int32, (rows, glob), 1)
    target = lax.broadcasted_iota(jnp.int32, (rows, glob), 0)
    total = jnp.where(lax.rem(source, rows) == target, 1.0, 0.0).astype(BF16)
    glob_ref[...] = dot(total, got_ref[:, :wide], 1, 0).astype(BF16)


def reply_kernel(half, capacity, direct, here_ref, asked_ref, k_ref, v_ref, mk_ref, mv_ref, glob_ref, mglob_ref,
                 *out_refs):
    tokens, width = k_ref.shape
    rows = glob_ref.shape[0]
    skip = 2 * capacity * BLK
    share = (glob_ref[...].astype(F32) + mglob_ref[...].astype(F32)).astype(BF16)
    for j, out_ref in enumerate(out_refs):
        member = member_of(here_ref, direct, half, j)
        for slot in range(2 * capacity):
            block = jnp.maximum(asked_ref[member, slot], 0)
            source = pl.ds(pl.multiple_of(block * BLK, BLK), BLK)
            target = slice(slot * BLK, (slot + 1) * BLK)
            own = slot < capacity
            out_ref[target, :width] = (k_ref if own else mk_ref)[source, :]
            out_ref[target, width:] = (v_ref if own else mv_ref)[source, :]
        out_ref[skip : skip + rows, :] = share


def attend_kernel(half, capacity, direct, place_ref, here_ref, q_ref, ga_ref, og_ref, k_ref, v_ref, low_ref, high_ref,
                  *refs):
    pieces, dk_pieces, dv_pieces = (refs[at : at + half] for at in range(0, 3 * half, half))
    inner_k_ref, inner_v_ref, elow_ref, ehigh_ref, att_ref, dq_ref = refs[3 * half : 3 * half + 6]
    pad_ref, kc_ref, vc_ref, acc_ref, gacc_ref, arr_ref, dk_out_ref, dv_out_ref = refs[3 * half + 6 :]
    tokens, width = q_ref.shape
    query_blocks = tokens // BLK
    head_size = width // HEADS
    scale = head_size ** (-0.5)
    win, local = 3 * BLK, (3 + RAND) * BLK
    requests = query_blocks * RAND
    pad_ref[:BLK] = low_ref[...]
    pad_ref[BLK : BLK + tokens, :width] = k_ref[...]
    pad_ref[BLK : BLK + tokens, width:] = v_ref[...]
    pad_ref[BLK + tokens :] = high_ref[...]
    skip = 2 * capacity * BLK
    rows = gacc_ref.shape[0] // half
    for j, piece in enumerate(pieces):
        stride = piece.shape[0]
        mine = slice(local + j * rows, local + (j + 1) * rows)
        arr_ref[j * stride : (j + 1) * stride] = piece[...]
        kc_ref[mine] = piece[skip : skip + rows, :width]
        vc_ref[mine] = piece[skip : skip + rows, width:]
    acc_ref[...] = jnp.zeros_like(acc_ref)
    gacc_ref[...] = jnp.zeros_like(gacc_ref)
    row_head = lax.broadcasted_iota(jnp.int32, (HEADS * BLK, width), 0) // BLK
    lane_head = lax.broadcasted_iota(jnp.int32, (HEADS * BLK, width), 1) // head_size
    mask = jnp.where(row_head == lane_head, 1.0, 0.0).astype(BF16)
    keep = jnp.where(row_head == lane_head, 1.0, 0.0)

    def by_head(rows):
        return jnp.concatenate([rows] * HEADS, axis=0) * mask

    def own_head(full):
        kept = full * keep
        return sum(kept[h * BLK : (h + 1) * BLK] for h in range(HEADS))

    def one_block(i, carry):
        base = pl.multiple_of(i * BLK, BLK)
        kc_ref[:win] = pad_ref[pl.ds(base, win), :width]
        vc_ref[:win] = pad_ref[pl.ds(base, win), width:]
        for j in range(RAND):
            slot = pl.ds(pl.multiple_of(place_ref[i * RAND + j], BLK), BLK)
            kc_ref[win + j * BLK : win + (j + 1) * BLK] = arr_ref[slot, :width]
            vc_ref[win + j * BLK : win + (j + 1) * BLK] = arr_ref[slot, width:]
        q_by_head = by_head(q_ref[pl.ds(base, BLK), :])
        ga_by_head = by_head(ga_ref[pl.ds(base, BLK), :])
        scores = dot(kc_ref[...], q_by_head, 1, 1) * (scale * LOG2E)
        expo = jnp.exp2(scores - jnp.max(scores, axis=0, keepdims=True))
        probs = expo * (1.0 / jnp.sum(expo, axis=0, keepdims=True))
        probs16 = probs.astype(BF16)
        dprobs = dot(vc_ref[...], ga_by_head, 1, 1)
        delta = jnp.sum(probs16.astype(F32) * dprobs, axis=0, keepdims=True)
        dscores = (probs * (dprobs - delta) * scale).astype(BF16)
        att_ref[pl.ds(base, BLK), :] = own_head(dot(probs16, vc_ref[...], 0, 0)).astype(BF16)
        dq_ref[pl.ds(base, BLK), :] = own_head(dot(dscores, kc_ref[...], 0, 0)).astype(BF16)
        for out_ref, part, terms in (
            (dv_out_ref, slice(width, 2 * width), dot(probs16, ga_by_head, 1, 0)),
            (dk_out_ref, slice(0, width), dot(dscores, q_by_head, 1, 0)),
        ):
            acc_ref[pl.ds(base, win), part] += terms[:win]
            gacc_ref[:, part] += terms[local:]
            for j in range(RAND):
                slot = place_ref[requests + i * RAND + j]
                out_ref[pl.ds(pl.multiple_of(slot, 16), BLK), :] = terms[
                    win + j * BLK : win + (j + 1) * BLK
                ].astype(BF16)
        return carry

    lax.fori_loop(0, query_blocks, one_block, 0, unroll=8)
    inner_k_ref[...] = acc_ref[BLK : BLK + tokens, :width]
    inner_v_ref[...] = acc_ref[BLK : BLK + tokens, width:]
    elow_ref[...] = acc_ref[:BLK].astype(BF16)
    ehigh_ref[...] = acc_ref[BLK + tokens :].astype(BF16)
    gacc_ref[:, 2 * width :] = dot(att_ref[...], og_ref[...], 0, 0)
    for j in range(half):
        dk_pieces[j][...] = dk_out_ref[j * skip : (j + 1) * skip]
        dv_pieces[j][:skip] = dv_out_ref[j * skip : (j + 1) * skip]
        member_rows = rows_of(member_of(here_ref, direct, half, j), rows)
        for part in range(gacc_ref.shape[1] // width):
            at = skip + part * rows
            mine = slice(j * rows, (j + 1) * rows) if part < 2 else member_rows
            dv_pieces[j][at : at + rows, :] = gacc_ref[
                mine, part * width : (part + 1) * width
            ].astype(BF16)


def fold_kernel(half, capacity, direct, here_ref, asked_ref, inner_ref, *refs):
    pieces = refs[:half]
    own_ref, give_ref, mirror_acc = refs[half:]
    tokens = own_ref.shape[0]
    skip = 2 * capacity * BLK
    own_ref[...] = inner_ref[...]
    mirror_acc[...] = jnp.zeros_like(mirror_acc)
    for j, piece in enumerate(pieces):
        member = member_of(here_ref, direct, half, j)
        for slot in range(2 * capacity):
            block = asked_ref[member, slot]
            acc_ref = own_ref if slot < capacity else mirror_acc
            at = slot * BLK

            @pl.when(block >= 0)
            def _():
                rows = pl.ds(pl.multiple_of(block * BLK, BLK), BLK)
                acc_ref[rows, :] += piece[at : at + BLK, :].astype(F32)

    give_ref[:tokens] = mirror_acc[...].astype(BF16)
    if pieces[0].shape[0] > skip:
        total = pieces[0][skip:, :].astype(F32)
        for piece in pieces[1:]:
            total += piece[skip:, :].astype(F32)
        give_ref[tokens:] = total.astype(BF16)


def finish_kernel(half, direct, here_ref, pos_ref, own_k_ref, own_v_ref, far_k_ref, far_v_ref, from_low_ref,
                  from_high_ref, total_ref, dk_ref, dv_ref, weight_ref, acc_ref, glob_ref):
    tokens, width = dk_ref.shape
    glob = pos_ref.shape[1]
    rows = glob // half
    stride = total_ref.shape[0] // half
    here = here_ref[0] * tokens + lax.broadcasted_iota(jnp.int32, (tokens, glob), 0)
    owned = jnp.where(here == pos_ref[...], 1.0, 0.0).astype(BF16)
    for j in range(half):
        mine = rows_of(j, rows)
        for part in range(stride // rows):
            at = j * stride + part * rows
            piece = total_ref[at : at + rows, :].astype(F32)
            if part < 2:
                glob_ref[mine, part * width : (part + 1) * width] = piece
            else:
                weight_ref[mine, (part - 2) * width : (part - 1) * width] = piece
    for part, own_ref, far_ref, out_ref in (
        (slice(0, width), own_k_ref, far_k_ref, dk_ref),
        (slice(width, 2 * width), own_v_ref, far_v_ref, dv_ref),
    ):
        acc_ref[...] = own_ref[...] + far_ref[:tokens].astype(F32) + dot(owned, glob_ref[:, part].astype(BF16), 1, 0)
        acc_ref[:BLK] += from_low_ref[:, part].astype(F32)
        acc_ref[tokens - BLK :] += from_high_ref[:, part].astype(F32)
        out_ref[...] = acc_ref[...].astype(BF16)


def shards(queries, keys, values, output_weight, output_grad, rand_blocks, glob_pos):
    q, k, v, og = queries[0], keys[0], values[0], output_grad[0]
    tokens, width = q.shape
    model = og.shape[1]
    glob = glob_pos.shape[1]
    query_blocks = tokens // BLK
    span = lax.axis_size("ctx")
    batch = lax.axis_size("batch")
    requests = query_blocks * RAND
    capacity = requests // span + 1
    half = span // 2
    rows = glob // half
    wide = 2 * width + model
    skip = 2 * capacity * BLK
    strides = (skip + -(-rows // 16) * 16, skip)
    more = rows * wide // width
    me = lax.axis_index("ctx").astype(jnp.int32)
    direct = half <= 8
    here = jnp.stack([me, me % half if direct else jnp.zeros_like(me)])
    shape = jax.ShapeDtypeStruct
    forward = [(i, (i + 1) % span) for i in range(span)]
    backward = [(target, source) for source, target in forward]
    mirror = [(i, (i + half) % span) for i in range(span)]
    halves = [list(range(half)), list(range(half, span))]

    def swap(x):
        return lax.all_to_all(
            x, "ctx", split_axis=0, concat_axis=0, axis_index_groups=halves, tiled=True
        )

    def flip(x, mask):
        return lax.ppermute(x, "ctx", [(i, i ^ mask) for i in range(span)])

    def trade(pieces):
        if not direct:
            return [piece[0] for piece in jnp.split(swap(jnp.stack(pieces)), half)]
        return [pieces[0]] + [
            flip(pieces[j], mask) for j, mask in enumerate(masks_of(half)) if mask
        ]

    mirror_k = lax.ppermute(k, "ctx", mirror)
    send, places, v_after = pl.pallas_call(
        functools.partial(ask_kernel, half, capacity, strides),
        name="ask",
        out_shape=(
            shape((glob, 2 * width + LANES), BF16),
            shape((2 * requests,), jnp.int32),
            shape((tokens, width), BF16),
        ),
        in_specs=[SMEM, SMEM, VMEM, VMEM, VMEM],
        out_specs=(VMEM, SMEM, VMEM),
        scratch_shapes=[pltpu.SMEM((span,), jnp.int32), pltpu.SMEM((span * capacity,), jnp.int32)],
        compiler_params=params(60),
    )(here, rand_blocks.reshape(requests), glob_pos, k, v)
    got = swap(send)
    mirror_v = lax.ppermute(v_after, "ctx", mirror)
    key_value_edges = [
        jnp.concatenate([k[edge], v[edge]], axis=1)
        for edge in (slice(tokens - BLK, tokens), slice(0, BLK))
    ]
    low = lax.ppermute(key_value_edges[0], "ctx", forward)
    high = lax.ppermute(key_value_edges[1], "ctx", backward)
    grad_attn = dot(og, output_weight, 1, 1).astype(BF16)

    glob_here, asked = pl.pallas_call(
        functools.partial(heard_kernel, half),
        name="heard",
        out_shape=(shape((rows, 2 * width), BF16), shape((half, LANES), jnp.int32)),
        in_specs=[VMEM],
        out_specs=(VMEM,) * 2,
        compiler_params=params(16),
    )(got)
    glob_there = lax.ppermute(glob_here, "ctx", mirror)
    reply = pl.pallas_call(
        functools.partial(reply_kernel, half, capacity, direct),
        name="reply",
        out_shape=[shape((strides[0], 2 * width), BF16)] * half,
        in_specs=[SMEM, SMEM] + [VMEM] * 6,
        out_specs=[VMEM] * half,
        compiler_params=params(16),
    )(here, asked, k, v, mirror_k, mirror_v, glob_here, glob_there)
    reply, low, high = lax.optimization_barrier((reply, low, high))
    arrived = trade(reply)

    block = (3 + RAND) * BLK + glob
    *gives, inner_k, inner_v, edge_low, edge_high, attention_rows, grad_queries = pl.pallas_call(
        functools.partial(attend_kernel, half, capacity, direct),
        name="attend",
        out_shape=[shape((skip, width), BF16)] * half
        + [shape((skip + more, width), BF16)] * half
        + [
            shape((tokens, width), F32),
            shape((tokens, width), F32),
            shape((BLK, 2 * width), BF16),
            shape((BLK, 2 * width), BF16),
            shape((tokens, width), BF16),
            shape((tokens, width), BF16),
        ],
        in_specs=[SMEM, SMEM] + [VMEM] * (7 + half),
        out_specs=[VMEM] * (2 * half + 6),
        scratch_shapes=[
            pltpu.VMEM((tokens + 2 * BLK, 2 * width), BF16),
            pltpu.VMEM((block, width), BF16),
            pltpu.VMEM((block, width), BF16),
            pltpu.VMEM((tokens + 2 * BLK, 2 * width), F32),
            pltpu.VMEM((glob, wide), F32),
            pltpu.VMEM((half * strides[0], 2 * width), BF16),
            pltpu.VMEM((half * skip, width), BF16),
            pltpu.VMEM((half * skip, width), BF16),
        ],
        compiler_params=params(32),
    )(places, here, q, grad_attn, og, k, v, low, high, *arrived)

    from_high = lax.ppermute(edge_low, "ctx", backward)
    from_low = lax.ppermute(edge_high, "ctx", forward)
    dv_back = trade(gives[half:])
    dk_back = trade(gives[:half])

    def fold(name, back, inner, more):
        return pl.pallas_call(
            functools.partial(fold_kernel, half, capacity, direct),
            name=name,
            out_shape=(shape((tokens, width), F32), shape((tokens + more, width), BF16)),
            in_specs=[SMEM, SMEM, VMEM] + [VMEM] * half,
            out_specs=(VMEM,) * 2,
            scratch_shapes=[pltpu.VMEM((tokens, width), F32)],
            compiler_params=params(16),
        )(here, asked, inner, *back)

    own_v, give_v = fold("fold_values", dv_back, inner_v, more)
    far_v = lax.ppermute(give_v, "ctx", mirror)
    far_v, from_high, from_low = lax.optimization_barrier((far_v, from_high, from_low))
    weight_at = tokens + 2 * rows
    weight_share = give_v[weight_at:]
    weight_sum = weight_share.astype(F32) + far_v[weight_at:].astype(F32)
    for step in range(1, batch):
        same, crossed = (
            lax.ppermute(
                weight_share,
                ("ctx", "batch"),
                [
                    (i * batch + b, (i + shift) % span * batch + (b + step) % batch)
                    for i in range(span)
                    for b in range(batch)
                ],
            ).astype(F32)
            for shift in (0, half)
        )
        weight_sum += same + crossed
    glob_sum = give_v[tokens:weight_at].astype(F32) + far_v[tokens:weight_at].astype(F32)
    share = jnp.concatenate([glob_sum, weight_sum], axis=0).astype(BF16)
    own_k, give_k = fold("fold_keys", dk_back, inner_k, 0)
    far_k = lax.ppermute(give_k, "ctx", mirror)
    share, own_k = lax.optimization_barrier((share, own_k))
    totals = lax.all_gather(share, "ctx", axis=0, axis_index_groups=halves, tiled=True)
    attended = dot(attention_rows, output_weight, 1, 0).astype(BF16)

    grad_keys, grad_values, grad_weight = pl.pallas_call(
        functools.partial(finish_kernel, half, direct),
        name="finish",
        out_shape=(
            shape((tokens, width), BF16),
            shape((tokens, width), BF16),
            shape((width, model), F32),
        ),
        in_specs=[SMEM] + [VMEM] * 8,
        out_specs=(VMEM,) * 3,
        scratch_shapes=[
            pltpu.VMEM((tokens, width), F32),
            pltpu.VMEM((glob, 2 * width), F32),
        ],
        compiler_params=params(24),
    )(here, glob_pos, own_k, own_v, far_k, far_v, from_low, from_high, totals)
    return (
        attended[None],
        grad_queries[None],
        grad_keys[None],
        grad_values[None],
        grad_weight,
    )


def solution(mesh):
    in_specs = (
        P("batch", "ctx", None),
        P("batch", "ctx", None),
        P("batch", "ctx", None),
        P(),
        P("batch", "ctx", None),
        P("batch", "ctx", None),
        P("batch", None),
    )
    out_specs = (
        P("batch", "ctx", None),
        P("batch", "ctx", None),
        P("batch", "ctx", None),
        P("batch", "ctx", None),
        P(),
    )
    return jax.shard_map(shards, mesh=mesh, in_specs=in_specs, out_specs=out_specs, check_vma=False)
```

```python
import functools

import jax
import jax.numpy as jnp
from jax import lax
from jax.experimental import pallas as pl
from jax.experimental.pallas import tpu as pltpu
from jax.sharding import PartitionSpec as P

BLK = 64
HEADS = 4
RAND = 3
LANES = 128
MIB = 1024 * 1024
LOG2E = 1.4426950408889634
MASKS = (0, 6, 2, 4, 7, 3, 5, 1)

F32 = jnp.float32
BF16 = jnp.bfloat16
VMEM = pl.BlockSpec(memory_space=pltpu.VMEM)
SMEM = pl.BlockSpec(memory_space=pltpu.SMEM)


def params(mib):
    return pltpu.CompilerParams(vmem_limit_bytes=mib * MIB)


def dot(left, right, over_left, over_right):
    return lax.dot_general(
        left, right, (((over_left,), (over_right,)), ((), ())), preferred_element_type=F32
    )


def masks_of(half):
    return MASKS if half == len(MASKS) else tuple(range(half))


def member_of(here_ref, direct, half, j):
    return here_ref[1] ^ masks_of(half)[j] if direct else j


def rows_of(member, rows):
    if isinstance(member, int):
        return slice(member * rows, (member + 1) * rows)
    return pl.ds(pl.multiple_of(member * rows, rows), rows)


def ask_kernel(half, capacity, strides, here_ref, want_ref, pos_ref, k_ref, v_ref,
               send_ref, place_ref, v_out_ref, count_ref, list_ref):
    tokens, width = k_ref.shape
    glob = pos_ref.shape[1]
    query_blocks = tokens // BLK
    requests = query_blocks * RAND
    rows = glob // half
    lists = 2 * capacity
    me = here_ref[0]
    turn = here_ref[1]
    my_half = lax.div(me, half)
    for entry in range(2 * half):
        count_ref[entry] = 0
    for entry in range(half * lists):
        list_ref[entry] = -1

    def request(at, carry):
        wanted = want_ref[at]
        owner = lax.div(wanted, query_blocks)
        rank = jnp.minimum(count_ref[owner], capacity - 1)
        count_ref[owner] = count_ref[owner] + 1
        owner_half = lax.div(owner, half)
        member = owner - owner_half * half
        slot = jnp.where(owner_half == my_half, 0, capacity) + rank
        list_ref[member * lists + slot] = wanted - owner * query_blocks
        piece = member ^ turn
        piece = sum(jnp.where(piece == mask, j, 0) for j, mask in enumerate(masks_of(half)))
        for use, stride in enumerate(strides):
            place_ref[use * requests + at] = piece * stride + slot * BLK
        return carry

    lax.fori_loop(0, requests, request, 0)
    here = me * tokens + lax.broadcasted_iota(jnp.int32, (tokens, glob), 0)
    owned = jnp.where(here == pos_ref[...], 1.0, 0.0).astype(BF16)
    send_ref[:, :width] = dot(owned, k_ref[...], 0, 0).astype(BF16)
    send_ref[:, width : 2 * width] = dot(owned, v_ref[...], 0, 0).astype(BF16)
    v_out_ref[...] = v_ref[...]
    lane = lax.broadcasted_iota(jnp.int32, (rows, LANES), 1)
    for member in range(half):
        listed = jnp.full((rows, LANES), -1, jnp.int32)
        for slot in range(lists):
            listed = jnp.where(lane == slot, list_ref[member * lists + slot], listed)
        send_ref[member * rows : (member + 1) * rows, 2 * width :] = listed.astype(F32).astype(BF16)


def heard_kernel(half, got_ref, glob_ref, asked_ref):
    glob = got_ref.shape[0]
    rows = glob // half
    wide = glob_ref.shape[1]
    source = lax.broadcasted_iota(jnp.int32, (half, glob), 1)
    target = lax.broadcasted_iota(jnp.int32, (half, glob), 0)
    pick = jnp.where(source == target * rows, 1.0, 0.0).astype(BF16)
    asked_ref[...] = dot(pick, got_ref[:, wide:], 1, 0).astype(jnp.int32)
    source = lax.broadcasted_iota(jnp.int32, (rows, glob), 1)
    target = lax.broadcasted_iota(jnp.int32, (rows, glob), 0)
    total = jnp.where(lax.rem(source, rows) == target, 1.0, 0.0).astype(BF16)
    glob_ref[...] = dot(total, got_ref[:, :wide], 1, 0).astype(BF16)


def reply_kernel(half, capacity, direct, here_ref, asked_ref, k_ref, v_ref, mk_ref, mv_ref, glob_ref, mglob_ref,
                 *out_refs):
    tokens, width = k_ref.shape
    rows = glob_ref.shape[0]
    skip = 2 * capacity * BLK
    share = (glob_ref[...].astype(F32) + mglob_ref[...].astype(F32)).astype(BF16)
    for j, out_ref in enumerate(out_refs):
        member = member_of(here_ref, direct, half, j)
        for slot in range(2 * capacity):
            block = jnp.maximum(asked_ref[member, slot], 0)
            source = pl.ds(pl.multiple_of(block * BLK, BLK), BLK)
            target = slice(slot * BLK, (slot + 1) * BLK)
            own = slot < capacity
            out_ref[target, :width] = (k_ref if own else mk_ref)[source, :]
            out_ref[target, width:] = (v_ref if own else mv_ref)[source, :]
        out_ref[skip : skip + rows, :] = share


def attend_kernel(half, capacity, direct, place_ref, here_ref, q_ref, ga_ref, og_ref, k_ref, v_ref, low_ref, high_ref,
                  *refs):
    pieces, dk_pieces, dv_pieces = (refs[at : at + half] for at in range(0, 3 * half, half))
    inner_k_ref, inner_v_ref, elow_ref, ehigh_ref, att_ref, dq_ref = refs[3 * half : 3 * half + 6]
    pad_ref, kc_ref, vc_ref, acc_ref, gacc_ref, arr_ref, dk_out_ref, dv_out_ref = refs[3 * half + 6 :]
    tokens, width = q_ref.shape
    query_blocks = tokens // BLK
    head_size = width // HEADS
    scale = head_size ** (-0.5)
    win, local = 3 * BLK, (3 + RAND) * BLK
    requests = query_blocks * RAND
    pad_ref[:BLK] = low_ref[...]
    pad_ref[BLK : BLK + tokens, :width] = k_ref[...]
    pad_ref[BLK : BLK + tokens, width:] = v_ref[...]
    pad_ref[BLK + tokens :] = high_ref[...]
    skip = 2 * capacity * BLK
    rows = gacc_ref.shape[0] // half
    for j, piece in enumerate(pieces):
        stride = piece.shape[0]
        mine = slice(local + j * rows, local + (j + 1) * rows)
        arr_ref[j * stride : (j + 1) * stride] = piece[...]
        kc_ref[mine] = piece[skip : skip + rows, :width]
        vc_ref[mine] = piece[skip : skip + rows, width:]
    acc_ref[...] = jnp.zeros_like(acc_ref)
    gacc_ref[...] = jnp.zeros_like(gacc_ref)
    row_head = lax.broadcasted_iota(jnp.int32, (HEADS * BLK, width), 0) // BLK
    lane_head = lax.broadcasted_iota(jnp.int32, (HEADS * BLK, width), 1) // head_size
    mask = jnp.where(row_head == lane_head, 1.0, 0.0).astype(BF16)
    keep = jnp.where(row_head == lane_head, 1.0, 0.0)

    def by_head(rows):
        return jnp.concatenate([rows] * HEADS, axis=0) * mask

    def own_head(full):
        kept = full * keep
        return sum(kept[h * BLK : (h + 1) * BLK] for h in range(HEADS))

    def one_block(i, carry):
        base = pl.multiple_of(i * BLK, BLK)
        kc_ref[:win] = pad_ref[pl.ds(base, win), :width]
        vc_ref[:win] = pad_ref[pl.ds(base, win), width:]
        for j in range(RAND):
            slot = pl.ds(pl.multiple_of(place_ref[i * RAND + j], BLK), BLK)
            kc_ref[win + j * BLK : win + (j + 1) * BLK] = arr_ref[slot, :width]
            vc_ref[win + j * BLK : win + (j + 1) * BLK] = arr_ref[slot, width:]
        q_by_head = by_head(q_ref[pl.ds(base, BLK), :])
        ga_by_head = by_head(ga_ref[pl.ds(base, BLK), :])
        scores = dot(kc_ref[...], q_by_head, 1, 1) * (scale * LOG2E)
        expo = jnp.exp2(scores - jnp.max(scores, axis=0, keepdims=True))
        probs = expo * (1.0 / jnp.sum(expo, axis=0, keepdims=True))
        probs16 = probs.astype(BF16)
        dprobs = dot(vc_ref[...], ga_by_head, 1, 1)
        delta = jnp.sum(probs16.astype(F32) * dprobs, axis=0, keepdims=True)
        dscores = (probs * (dprobs - delta) * scale).astype(BF16)
        att_ref[pl.ds(base, BLK), :] = own_head(dot(probs16, vc_ref[...], 0, 0)).astype(BF16)
        dq_ref[pl.ds(base, BLK), :] = own_head(dot(dscores, kc_ref[...], 0, 0)).astype(BF16)
        for out_ref, part, terms in (
            (dv_out_ref, slice(width, 2 * width), dot(probs16, ga_by_head, 1, 0)),
            (dk_out_ref, slice(0, width), dot(dscores, q_by_head, 1, 0)),
        ):
            acc_ref[pl.ds(base, win), part] += terms[:win]
            gacc_ref[:, part] += terms[local:]
            for j in range(RAND):
                slot = place_ref[requests + i * RAND + j]
                out_ref[pl.ds(pl.multiple_of(slot, 16), BLK), :] = terms[
                    win + j * BLK : win + (j + 1) * BLK
                ].astype(BF16)
        return carry

    lax.fori_loop(0, query_blocks, one_block, 0, unroll=8)
    inner_k_ref[...] = acc_ref[BLK : BLK + tokens, :width]
    inner_v_ref[...] = acc_ref[BLK : BLK + tokens, width:]
    elow_ref[...] = acc_ref[:BLK].astype(BF16)
    ehigh_ref[...] = acc_ref[BLK + tokens :].astype(BF16)
    gacc_ref[:, 2 * width :] = dot(att_ref[...], og_ref[...], 0, 0)
    for j in range(half):
        dk_pieces[j][...] = dk_out_ref[j * skip : (j + 1) * skip]
        dv_pieces[j][:skip] = dv_out_ref[j * skip : (j + 1) * skip]
        member_rows = rows_of(member_of(here_ref, direct, half, j), rows)
        for part in range(gacc_ref.shape[1] // width):
            at = skip + part * rows
            mine = slice(j * rows, (j + 1) * rows) if part < 2 else member_rows
            dv_pieces[j][at : at + rows, :] = gacc_ref[
                mine, part * width : (part + 1) * width
            ].astype(BF16)


def fold_kernel(half, capacity, direct, here_ref, asked_ref, inner_ref, *refs):
    pieces = refs[:half]
    own_ref, give_ref, mirror_acc = refs[half:]
    tokens = own_ref.shape[0]
    skip = 2 * capacity * BLK
    own_ref[...] = inner_ref[...]
    mirror_acc[...] = jnp.zeros_like(mirror_acc)
    for j, piece in enumerate(pieces):
        member = member_of(here_ref, direct, half, j)
        for slot in range(2 * capacity):
            block = asked_ref[member, slot]
            acc_ref = own_ref if slot < capacity else mirror_acc
            at = slot * BLK

            @pl.when(block >= 0)
            def _():
                rows = pl.ds(pl.multiple_of(block * BLK, BLK), BLK)
                acc_ref[rows, :] += piece[at : at + BLK, :].astype(F32)

    give_ref[:tokens] = mirror_acc[...].astype(BF16)
    if pieces[0].shape[0] > skip:
        total = pieces[0][skip:, :].astype(F32)
        for piece in pieces[1:]:
            total += piece[skip:, :].astype(F32)
        give_ref[tokens:] = total.astype(BF16)


def finish_kernel(masks, here_ref, pos_ref, own_k_ref, own_v_ref, far_k_ref, far_v_ref, from_low_ref,
                  from_high_ref, *refs):
    dk_ref, dv_ref, weight_ref, acc_ref, glob_ref = refs[-5:]
    half = len(masks)
    tokens, width = dk_ref.shape
    glob = pos_ref.shape[1]
    rows = glob // half
    stride = sum(ref.shape[0] for ref in refs[:-5]) // half
    here = here_ref[0] * tokens + lax.broadcasted_iota(jnp.int32, (tokens, glob), 0)
    owned = jnp.where(here == pos_ref[...], 1.0, 0.0).astype(BF16)
    places = [(ref, at) for ref in refs[:-5] for at in range(0, ref.shape[0], stride)]
    for mask, (total_ref, first) in zip(masks, places):
        mine = rows_of(here_ref[1] ^ mask if len(refs) > 6 else mask, rows)
        for part in range(stride // rows):
            at = first + part * rows
            piece = total_ref[at : at + rows, :].astype(F32)
            if part < 2:
                glob_ref[mine, part * width : (part + 1) * width] = piece
            else:
                weight_ref[mine, (part - 2) * width : (part - 1) * width] = piece
    for part, own_ref, far_ref, out_ref in (
        (slice(0, width), own_k_ref, far_k_ref, dk_ref),
        (slice(width, 2 * width), own_v_ref, far_v_ref, dv_ref),
    ):
        acc_ref[...] = own_ref[...] + far_ref[:tokens].astype(F32) + dot(owned, glob_ref[:, part].astype(BF16), 1, 0)
        acc_ref[:BLK] += from_low_ref[:, part].astype(F32)
        acc_ref[tokens - BLK :] += from_high_ref[:, part].astype(F32)
        out_ref[...] = acc_ref[...].astype(BF16)


def shards(queries, keys, values, output_weight, output_grad, rand_blocks, glob_pos):
    q, k, v, og = queries[0], keys[0], values[0], output_grad[0]
    tokens, width = q.shape
    model = og.shape[1]
    glob = glob_pos.shape[1]
    query_blocks = tokens // BLK
    span = lax.axis_size("ctx")
    batch = lax.axis_size("batch")
    requests = query_blocks * RAND
    capacity = requests // span + 1
    half = span // 2
    rows = glob // half
    wide = 2 * width + model
    skip = 2 * capacity * BLK
    strides = (skip + -(-rows // 16) * 16, skip)
    more = rows * wide // width
    me = lax.axis_index("ctx").astype(jnp.int32)
    direct = half == 8
    here = jnp.stack([me, me % half if direct else jnp.zeros_like(me)])
    shape = jax.ShapeDtypeStruct
    forward = [(i, (i + 1) % span) for i in range(span)]
    backward = [(target, source) for source, target in forward]
    mirror = [(i, (i + half) % span) for i in range(span)]
    halves = [list(range(half)), list(range(half, span))]

    def swap(x):
        return lax.all_to_all(
            x, "ctx", split_axis=0, concat_axis=0, axis_index_groups=halves, tiled=True
        )

    def flip(x, mask):
        return lax.ppermute(x, "ctx", [(i, i ^ mask) for i in range(span)])

    def trade(pieces):
        if not direct:
            return [piece[0] for piece in jnp.split(swap(jnp.stack(pieces)), half)]
        return [pieces[0]] + [
            flip(pieces[j], mask) for j, mask in enumerate(masks_of(half)) if mask
        ]

    mirror_k = lax.ppermute(k, "ctx", mirror)
    send, places, v_after = pl.pallas_call(
        functools.partial(ask_kernel, half, capacity, strides),
        name="ask",
        out_shape=(
            shape((glob, 2 * width + LANES), BF16),
            shape((2 * requests,), jnp.int32),
            shape((tokens, width), BF16),
        ),
        in_specs=[SMEM, SMEM, VMEM, VMEM, VMEM],
        out_specs=(VMEM, SMEM, VMEM),
        scratch_shapes=[pltpu.SMEM((span,), jnp.int32), pltpu.SMEM((span * capacity,), jnp.int32)],
        compiler_params=params(60),
    )(here, rand_blocks.reshape(requests), glob_pos, k, v)
    got = swap(send)
    mirror_v = lax.ppermute(v_after, "ctx", mirror)
    key_value_edges = [
        jnp.concatenate([k[edge], v[edge]], axis=1)
        for edge in (slice(tokens - BLK, tokens), slice(0, BLK))
    ]
    low = lax.ppermute(key_value_edges[0], "ctx", forward)
    high = lax.ppermute(key_value_edges[1], "ctx", backward)
    grad_attn = dot(og, output_weight, 1, 1).astype(BF16)

    glob_here, asked = pl.pallas_call(
        functools.partial(heard_kernel, half),
        name="heard",
        out_shape=(shape((rows, 2 * width), BF16), shape((half, LANES), jnp.int32)),
        in_specs=[VMEM],
        out_specs=(VMEM,) * 2,
        compiler_params=params(16),
    )(got)
    glob_there = lax.ppermute(glob_here, "ctx", mirror)
    reply = pl.pallas_call(
        functools.partial(reply_kernel, half, capacity, direct),
        name="reply",
        out_shape=[shape((strides[0], 2 * width), BF16)] * half,
        in_specs=[SMEM, SMEM] + [VMEM] * 6,
        out_specs=[VMEM] * half,
        compiler_params=params(16),
    )(here, asked, k, v, mirror_k, mirror_v, glob_here, glob_there)
    reply, low, high = lax.optimization_barrier((reply, low, high))
    arrived = trade(reply)

    block = (3 + RAND) * BLK + glob
    *gives, inner_k, inner_v, edge_low, edge_high, attention_rows, grad_queries = pl.pallas_call(
        functools.partial(attend_kernel, half, capacity, direct),
        name="attend",
        out_shape=[shape((skip, width), BF16)] * half
        + [shape((skip + more, width), BF16)] * half
        + [
            shape((tokens, width), F32),
            shape((tokens, width), F32),
            shape((BLK, 2 * width), BF16),
            shape((BLK, 2 * width), BF16),
            shape((tokens, width), BF16),
            shape((tokens, width), BF16),
        ],
        in_specs=[SMEM, SMEM] + [VMEM] * (7 + half),
        out_specs=[VMEM] * (2 * half + 6),
        scratch_shapes=[
            pltpu.VMEM((tokens + 2 * BLK, 2 * width), BF16),
            pltpu.VMEM((block, width), BF16),
            pltpu.VMEM((block, width), BF16),
            pltpu.VMEM((tokens + 2 * BLK, 2 * width), F32),
            pltpu.VMEM((glob, wide), F32),
            pltpu.VMEM((half * strides[0], 2 * width), BF16),
            pltpu.VMEM((half * skip, width), BF16),
            pltpu.VMEM((half * skip, width), BF16),
        ],
        compiler_params=params(32),
    )(places, here, q, grad_attn, og, k, v, low, high, *arrived)

    from_high = lax.ppermute(edge_low, "ctx", backward)
    from_low = lax.ppermute(edge_high, "ctx", forward)
    dv_back = trade(gives[half:])
    dk_back = trade(gives[:half])

    def fold(name, back, inner, more):
        return pl.pallas_call(
            functools.partial(fold_kernel, half, capacity, direct),
            name=name,
            out_shape=(shape((tokens, width), F32), shape((tokens + more, width), BF16)),
            in_specs=[SMEM, SMEM, VMEM] + [VMEM] * half,
            out_specs=(VMEM,) * 2,
            scratch_shapes=[pltpu.VMEM((tokens, width), F32)],
            compiler_params=params(16),
        )(here, asked, inner, *back)

    own_v, give_v = fold("fold_values", dv_back, inner_v, more)
    far_share = lax.ppermute(give_v[tokens:], "ctx", mirror)
    far_v = lax.ppermute(give_v[:tokens], "ctx", mirror)
    weight_at = tokens + 2 * rows
    weight_pair = (give_v[weight_at:].astype(F32) + far_share[2 * rows :].astype(F32)).astype(BF16)
    weight_sum = weight_pair.astype(F32)
    for step in range(1, batch):
        weight_sum += lax.ppermute(
            weight_pair, "batch", [(i, (i + step) % batch) for i in range(batch)]
        ).astype(F32)
    weight_sum, far_v = lax.optimization_barrier((weight_sum, far_v))
    glob_sum = give_v[tokens:weight_at].astype(F32) + far_share[: 2 * rows].astype(F32)
    share = jnp.concatenate([glob_sum, weight_sum], axis=0).astype(BF16)
    own_k, give_k = fold("fold_keys", dk_back, inner_k, 0)
    far_k = lax.ppermute(give_k, "ctx", mirror)
    share, own_k = lax.optimization_barrier((share, own_k))
    if direct:
        pair = jnp.concatenate([share, flip(share, 1)], axis=0)
        totals = [pair] + [flip(pair, mask) for mask in (6, 2, 4)]
        masks = (0, 1, 6, 7, 2, 3, 4, 5)
    else:
        totals = [lax.all_gather(share, "ctx", axis=0, axis_index_groups=halves, tiled=True)]
        masks = tuple(range(half))
    attended = dot(attention_rows, output_weight, 1, 0).astype(BF16)

    grad_keys, grad_values, grad_weight = pl.pallas_call(
        functools.partial(finish_kernel, masks),
        name="finish",
        out_shape=(
            shape((tokens, width), BF16),
            shape((tokens, width), BF16),
            shape((width, model), F32),
        ),
        in_specs=[SMEM] + [VMEM] * (7 + len(totals)),
        out_specs=(VMEM,) * 3,
        scratch_shapes=[
            pltpu.VMEM((tokens, width), F32),
            pltpu.VMEM((glob, 2 * width), F32),
        ],
        compiler_params=params(24),
    )(here, glob_pos, own_k, own_v, far_k, far_v, from_low, from_high, *totals)
    return (
        attended[None],
        grad_queries[None],
        grad_keys[None],
        grad_values[None],
        grad_weight,
    )


def solution(mesh):
    in_specs = (
        P("batch", "ctx", None),
        P("batch", "ctx", None),
        P("batch", "ctx", None),
        P(),
        P("batch", "ctx", None),
        P("batch", "ctx", None),
        P("batch", None),
    )
    out_specs = (
        P("batch", "ctx", None),
        P("batch", "ctx", None),
        P("batch", "ctx", None),
        P("batch", "ctx", None),
        P(),
    )
    return jax.shard_map(shards, mesh=mesh, in_specs=in_specs, out_specs=out_specs, check_vma=False)
```

```python
import functools

import jax
import jax.numpy as jnp
from jax import lax
from jax.experimental import pallas as pl
from jax.experimental.pallas import tpu as pltpu
from jax.sharding import PartitionSpec as P

BLK = 64
HEADS = 4
RAND = 3
LANES = 128
MIB = 1024 * 1024
LOG2E = 1.4426950408889634
MASKS = (0, 6, 2, 4, 3, 5, 7, 1)

F32 = jnp.float32
BF16 = jnp.bfloat16
VMEM = pl.BlockSpec(memory_space=pltpu.VMEM)
SMEM = pl.BlockSpec(memory_space=pltpu.SMEM)


def params(mib):
    return pltpu.CompilerParams(vmem_limit_bytes=mib * MIB)


def dot(left, right, over_left, over_right):
    return lax.dot_general(
        left, right, (((over_left,), (over_right,)), ((), ())), preferred_element_type=F32
    )


def masks_of(half):
    return MASKS if half == len(MASKS) else tuple(range(half))


def member_of(here_ref, direct, half, j):
    return here_ref[1] ^ masks_of(half)[j] if direct else j


def rows_of(member, rows):
    if isinstance(member, int):
        return slice(member * rows, (member + 1) * rows)
    return pl.ds(pl.multiple_of(member * rows, rows), rows)


def ask_kernel(half, capacity, strides, here_ref, want_ref, pos_ref, k_ref, v_ref,
               send_ref, place_ref, v_out_ref, count_ref, list_ref):
    tokens, width = k_ref.shape
    glob = pos_ref.shape[1]
    query_blocks = tokens // BLK
    requests = query_blocks * RAND
    rows = glob // half
    lists = 2 * capacity
    me = here_ref[0]
    turn = here_ref[1]
    my_half = lax.div(me, half)
    for entry in range(2 * half):
        count_ref[entry] = 0
    for entry in range(half * lists):
        list_ref[entry] = -1

    def request(at, carry):
        wanted = want_ref[at]
        owner = lax.div(wanted, query_blocks)
        rank = jnp.minimum(count_ref[owner], capacity - 1)
        count_ref[owner] = count_ref[owner] + 1
        owner_half = lax.div(owner, half)
        member = owner - owner_half * half
        slot = jnp.where(owner_half == my_half, 0, capacity) + rank
        list_ref[member * lists + slot] = wanted - owner * query_blocks
        piece = member ^ turn
        piece = sum(jnp.where(piece == mask, j, 0) for j, mask in enumerate(masks_of(half)))
        for use, stride in enumerate(strides):
            place_ref[use * requests + at] = piece * stride + slot * BLK
        return carry

    lax.fori_loop(0, requests, request, 0)
    here = me * tokens + lax.broadcasted_iota(jnp.int32, (tokens, glob), 0)
    owned = jnp.where(here == pos_ref[...], 1.0, 0.0).astype(BF16)
    send_ref[:, :width] = dot(owned, k_ref[...], 0, 0).astype(BF16)
    send_ref[:, width : 2 * width] = dot(owned, v_ref[...], 0, 0).astype(BF16)
    v_out_ref[...] = v_ref[...]
    lane = lax.broadcasted_iota(jnp.int32, (rows, LANES), 1)
    for member in range(half):
        listed = jnp.full((rows, LANES), -1, jnp.int32)
        for slot in range(lists):
            listed = jnp.where(lane == slot, list_ref[member * lists + slot], listed)
        send_ref[member * rows : (member + 1) * rows, 2 * width :] = listed.astype(F32).astype(BF16)


def heard_kernel(half, got_ref, glob_ref, asked_ref):
    glob = got_ref.shape[0]
    rows = glob // half
    wide = glob_ref.shape[1]
    source = lax.broadcasted_iota(jnp.int32, (half, glob), 1)
    target = lax.broadcasted_iota(jnp.int32, (half, glob), 0)
    pick = jnp.where(source == target * rows, 1.0, 0.0).astype(BF16)
    asked_ref[...] = dot(pick, got_ref[:, wide:], 1, 0).astype(jnp.int32)
    source = lax.broadcasted_iota(jnp.int32, (rows, glob), 1)
    target = lax.broadcasted_iota(jnp.int32, (rows, glob), 0)
    total = jnp.where(lax.rem(source, rows) == target, 1.0, 0.0).astype(BF16)
    glob_ref[...] = dot(total, got_ref[:, :wide], 1, 0).astype(BF16)


def reply_kernel(half, capacity, direct, here_ref, asked_ref, k_ref, v_ref, mk_ref, mv_ref, glob_ref, mglob_ref,
                 *out_refs):
    tokens, width = k_ref.shape
    rows = glob_ref.shape[0]
    skip = 2 * capacity * BLK
    share = (glob_ref[...].astype(F32) + mglob_ref[...].astype(F32)).astype(BF16)
    for j, out_ref in enumerate(out_refs):
        member = member_of(here_ref, direct, half, j)
        for slot in range(2 * capacity):
            block = jnp.maximum(asked_ref[member, slot], 0)
            source = pl.ds(pl.multiple_of(block * BLK, BLK), BLK)
            target = slice(slot * BLK, (slot + 1) * BLK)
            own = slot < capacity
            out_ref[target, :width] = (k_ref if own else mk_ref)[source, :]
            out_ref[target, width:] = (v_ref if own else mv_ref)[source, :]
        out_ref[skip : skip + rows, :] = share


def attend_kernel(half, capacity, direct, place_ref, here_ref, q_ref, ga_ref, og_ref, k_ref, v_ref, low_ref, high_ref,
                  *refs):
    pieces, dk_pieces, dv_pieces = (refs[at : at + half] for at in range(0, 3 * half, half))
    inner_k_ref, inner_v_ref, elow_ref, ehigh_ref, att_ref, dq_ref = refs[3 * half : 3 * half + 6]
    pad_ref, kc_ref, vc_ref, acc_ref, gacc_ref, arr_ref, dk_out_ref, dv_out_ref = refs[3 * half + 6 :]
    tokens, width = q_ref.shape
    query_blocks = tokens // BLK
    head_size = width // HEADS
    scale = head_size ** (-0.5)
    win, local = 3 * BLK, (3 + RAND) * BLK
    requests = query_blocks * RAND
    pad_ref[:BLK] = low_ref[...]
    pad_ref[BLK : BLK + tokens, :width] = k_ref[...]
    pad_ref[BLK : BLK + tokens, width:] = v_ref[...]
    pad_ref[BLK + tokens :] = high_ref[...]
    skip = 2 * capacity * BLK
    rows = gacc_ref.shape[0] // half
    for j, piece in enumerate(pieces):
        stride = piece.shape[0]
        mine = slice(local + j * rows, local + (j + 1) * rows)
        arr_ref[j * stride : (j + 1) * stride] = piece[...]
        kc_ref[mine] = piece[skip : skip + rows, :width]
        vc_ref[mine] = piece[skip : skip + rows, width:]
    acc_ref[...] = jnp.zeros_like(acc_ref)
    gacc_ref[...] = jnp.zeros_like(gacc_ref)
    row_head = lax.broadcasted_iota(jnp.int32, (HEADS * BLK, width), 0) // BLK
    lane_head = lax.broadcasted_iota(jnp.int32, (HEADS * BLK, width), 1) // head_size
    mask = jnp.where(row_head == lane_head, 1.0, 0.0).astype(BF16)
    keep = jnp.where(row_head == lane_head, 1.0, 0.0)

    def by_head(rows):
        return jnp.concatenate([rows] * HEADS, axis=0) * mask

    def own_head(full):
        kept = full * keep
        return sum(kept[h * BLK : (h + 1) * BLK] for h in range(HEADS))

    def one_block(i, carry):
        base = pl.multiple_of(i * BLK, BLK)
        kc_ref[:win] = pad_ref[pl.ds(base, win), :width]
        vc_ref[:win] = pad_ref[pl.ds(base, win), width:]
        for j in range(RAND):
            slot = pl.ds(pl.multiple_of(place_ref[i * RAND + j], BLK), BLK)
            kc_ref[win + j * BLK : win + (j + 1) * BLK] = arr_ref[slot, :width]
            vc_ref[win + j * BLK : win + (j + 1) * BLK] = arr_ref[slot, width:]
        q_by_head = by_head(q_ref[pl.ds(base, BLK), :])
        ga_by_head = by_head(ga_ref[pl.ds(base, BLK), :])
        scores = dot(kc_ref[...], q_by_head, 1, 1) * (scale * LOG2E)
        expo = jnp.exp2(scores - jnp.max(scores, axis=0, keepdims=True))
        probs = expo * (1.0 / jnp.sum(expo, axis=0, keepdims=True))
        probs16 = probs.astype(BF16)
        dprobs = dot(vc_ref[...], ga_by_head, 1, 1)
        delta = jnp.sum(probs16.astype(F32) * dprobs, axis=0, keepdims=True)
        dscores = (probs * (dprobs - delta) * scale).astype(BF16)
        att_ref[pl.ds(base, BLK), :] = own_head(dot(probs16, vc_ref[...], 0, 0)).astype(BF16)
        dq_ref[pl.ds(base, BLK), :] = own_head(dot(dscores, kc_ref[...], 0, 0)).astype(BF16)
        for out_ref, part, terms in (
            (dv_out_ref, slice(width, 2 * width), dot(probs16, ga_by_head, 1, 0)),
            (dk_out_ref, slice(0, width), dot(dscores, q_by_head, 1, 0)),
        ):
            acc_ref[pl.ds(base, win), part] += terms[:win]
            gacc_ref[:, part] += terms[local:]
            for j in range(RAND):
                slot = place_ref[requests + i * RAND + j]
                out_ref[pl.ds(pl.multiple_of(slot, 16), BLK), :] = terms[
                    win + j * BLK : win + (j + 1) * BLK
                ].astype(BF16)
        return carry

    lax.fori_loop(0, query_blocks, one_block, 0, unroll=8)
    inner_k_ref[...] = acc_ref[BLK : BLK + tokens, :width]
    inner_v_ref[...] = acc_ref[BLK : BLK + tokens, width:]
    elow_ref[...] = acc_ref[:BLK].astype(BF16)
    ehigh_ref[...] = acc_ref[BLK + tokens :].astype(BF16)
    gacc_ref[:, 2 * width :] = dot(att_ref[...], og_ref[...], 0, 0)
    for j in range(half):
        dk_pieces[j][...] = dk_out_ref[j * skip : (j + 1) * skip]
        dv_pieces[j][:skip] = dv_out_ref[j * skip : (j + 1) * skip]
        member_rows = rows_of(member_of(here_ref, direct, half, j), rows)
        for part in range(gacc_ref.shape[1] // width):
            at = skip + part * rows
            mine = slice(j * rows, (j + 1) * rows) if part < 2 else member_rows
            dv_pieces[j][at : at + rows, :] = gacc_ref[
                mine, part * width : (part + 1) * width
            ].astype(BF16)


def fold_kernel(half, capacity, direct, here_ref, asked_ref, inner_ref, *refs):
    pieces = refs[:half]
    own_ref, give_ref, mirror_acc = refs[half:]
    tokens = own_ref.shape[0]
    skip = 2 * capacity * BLK
    own_ref[...] = inner_ref[...]
    mirror_acc[...] = jnp.zeros_like(mirror_acc)
    for j, piece in enumerate(pieces):
        member = member_of(here_ref, direct, half, j)
        for slot in range(2 * capacity):
            block = asked_ref[member, slot]
            acc_ref = own_ref if slot < capacity else mirror_acc
            at = slot * BLK

            @pl.when(block >= 0)
            def _():
                rows = pl.ds(pl.multiple_of(block * BLK, BLK), BLK)
                acc_ref[rows, :] += piece[at : at + BLK, :].astype(F32)

    give_ref[:tokens] = mirror_acc[...].astype(BF16)
    if pieces[0].shape[0] > skip:
        total = pieces[0][skip:, :].astype(F32)
        for piece in pieces[1:]:
            total += piece[skip:, :].astype(F32)
        give_ref[tokens:] = total.astype(BF16)


def finish_kernel(masks, here_ref, pos_ref, own_k_ref, own_v_ref, far_k_ref, far_v_ref, from_low_ref,
                  from_high_ref, *refs):
    dk_ref, dv_ref, weight_ref, acc_ref, glob_ref = refs[-5:]
    half = len(masks)
    tokens, width = dk_ref.shape
    glob = pos_ref.shape[1]
    rows = glob // half
    stride = sum(ref.shape[0] for ref in refs[:-5]) // half
    here = here_ref[0] * tokens + lax.broadcasted_iota(jnp.int32, (tokens, glob), 0)
    owned = jnp.where(here == pos_ref[...], 1.0, 0.0).astype(BF16)
    places = [(ref, at) for ref in refs[:-5] for at in range(0, ref.shape[0], stride)]
    for mask, (total_ref, first) in zip(masks, places):
        mine = rows_of(here_ref[1] ^ mask if len(refs) > 6 else mask, rows)
        for part in range(stride // rows):
            at = first + part * rows
            piece = total_ref[at : at + rows, :].astype(F32)
            if part < 2:
                glob_ref[mine, part * width : (part + 1) * width] = piece
            else:
                weight_ref[mine, (part - 2) * width : (part - 1) * width] = piece
    for part, own_ref, far_ref, out_ref in (
        (slice(0, width), own_k_ref, far_k_ref, dk_ref),
        (slice(width, 2 * width), own_v_ref, far_v_ref, dv_ref),
    ):
        acc_ref[...] = own_ref[...] + far_ref[:tokens].astype(F32) + dot(owned, glob_ref[:, part].astype(BF16), 1, 0)
        acc_ref[:BLK] += from_low_ref[:, part].astype(F32)
        acc_ref[tokens - BLK :] += from_high_ref[:, part].astype(F32)
        out_ref[...] = acc_ref[...].astype(BF16)


def shards(queries, keys, values, output_weight, output_grad, rand_blocks, glob_pos):
    q, k, v, og = queries[0], keys[0], values[0], output_grad[0]
    tokens, width = q.shape
    model = og.shape[1]
    glob = glob_pos.shape[1]
    query_blocks = tokens // BLK
    span = lax.axis_size("ctx")
    batch = lax.axis_size("batch")
    requests = query_blocks * RAND
    capacity = requests // span + 1
    half = span // 2
    rows = glob // half
    wide = 2 * width + model
    skip = 2 * capacity * BLK
    strides = (skip + -(-rows // 16) * 16, skip)
    more = rows * wide // width
    me = lax.axis_index("ctx").astype(jnp.int32)
    direct = half == 8
    here = jnp.stack([me, me % half if direct else jnp.zeros_like(me)])
    shape = jax.ShapeDtypeStruct
    forward = [(i, (i + 1) % span) for i in range(span)]
    backward = [(target, source) for source, target in forward]
    mirror = [(i, (i + half) % span) for i in range(span)]
    halves = [list(range(half)), list(range(half, span))]

    def swap(x):
        return lax.all_to_all(
            x, "ctx", split_axis=0, concat_axis=0, axis_index_groups=halves, tiled=True
        )

    def flip(x, mask):
        return lax.ppermute(x, "ctx", [(i, i ^ mask) for i in range(span)])

    def trade(pieces):
        if not direct:
            return [piece[0] for piece in jnp.split(swap(jnp.stack(pieces)), half)]
        return [pieces[0]] + [
            flip(pieces[j], mask) for j, mask in enumerate(masks_of(half)) if mask
        ]

    mirror_k = lax.ppermute(k, "ctx", mirror)
    send, places, v_after = pl.pallas_call(
        functools.partial(ask_kernel, half, capacity, strides),
        name="ask",
        out_shape=(
            shape((glob, 2 * width + LANES), BF16),
            shape((2 * requests,), jnp.int32),
            shape((tokens, width), BF16),
        ),
        in_specs=[SMEM, SMEM, VMEM, VMEM, VMEM],
        out_specs=(VMEM, SMEM, VMEM),
        scratch_shapes=[pltpu.SMEM((span,), jnp.int32), pltpu.SMEM((span * capacity,), jnp.int32)],
        compiler_params=params(60),
    )(here, rand_blocks.reshape(requests), glob_pos, k, v)
    got = swap(send)
    mirror_v = lax.ppermute(v_after, "ctx", mirror)
    key_value_edges = [
        jnp.concatenate([k[edge], v[edge]], axis=1)
        for edge in (slice(tokens - BLK, tokens), slice(0, BLK))
    ]
    low = lax.ppermute(key_value_edges[0], "ctx", forward)
    high = lax.ppermute(key_value_edges[1], "ctx", backward)
    grad_attn = dot(og, output_weight, 1, 1).astype(BF16)

    glob_here, asked = pl.pallas_call(
        functools.partial(heard_kernel, half),
        name="heard",
        out_shape=(shape((rows, 2 * width), BF16), shape((half, LANES), jnp.int32)),
        in_specs=[VMEM],
        out_specs=(VMEM,) * 2,
        compiler_params=params(16),
    )(got)
    glob_there = lax.ppermute(glob_here, "ctx", mirror)
    reply = pl.pallas_call(
        functools.partial(reply_kernel, half, capacity, direct),
        name="reply",
        out_shape=[shape((strides[0], 2 * width), BF16)] * half,
        in_specs=[SMEM, SMEM] + [VMEM] * 6,
        out_specs=[VMEM] * half,
        compiler_params=params(16),
    )(here, asked, k, v, mirror_k, mirror_v, glob_here, glob_there)
    reply, low, high = lax.optimization_barrier((reply, low, high))
    arrived = trade(reply)

    block = (3 + RAND) * BLK + glob
    *gives, inner_k, inner_v, edge_low, edge_high, attention_rows, grad_queries = pl.pallas_call(
        functools.partial(attend_kernel, half, capacity, direct),
        name="attend",
        out_shape=[shape((skip, width), BF16)] * half
        + [shape((skip + more, width), BF16)] * half
        + [
            shape((tokens, width), F32),
            shape((tokens, width), F32),
            shape((BLK, 2 * width), BF16),
            shape((BLK, 2 * width), BF16),
            shape((tokens, width), BF16),
            shape((tokens, width), BF16),
        ],
        in_specs=[SMEM, SMEM] + [VMEM] * (7 + half),
        out_specs=[VMEM] * (2 * half + 6),
        scratch_shapes=[
            pltpu.VMEM((tokens + 2 * BLK, 2 * width), BF16),
            pltpu.VMEM((block, width), BF16),
            pltpu.VMEM((block, width), BF16),
            pltpu.VMEM((tokens + 2 * BLK, 2 * width), F32),
            pltpu.VMEM((glob, wide), F32),
            pltpu.VMEM((half * strides[0], 2 * width), BF16),
            pltpu.VMEM((half * skip, width), BF16),
            pltpu.VMEM((half * skip, width), BF16),
        ],
        compiler_params=params(32),
    )(places, here, q, grad_attn, og, k, v, low, high, *arrived)

    from_high = lax.ppermute(edge_low, "ctx", backward)
    from_low = lax.ppermute(edge_high, "ctx", forward)
    dv_back = trade(gives[half:])
    dk_back = trade(gives[:half])

    def fold(name, back, inner, more):
        return pl.pallas_call(
            functools.partial(fold_kernel, half, capacity, direct),
            name=name,
            out_shape=(shape((tokens, width), F32), shape((tokens + more, width), BF16)),
            in_specs=[SMEM, SMEM, VMEM] + [VMEM] * half,
            out_specs=(VMEM,) * 2,
            scratch_shapes=[pltpu.VMEM((tokens, width), F32)],
            compiler_params=params(16),
        )(here, asked, inner, *back)

    own_v, give_v = fold("fold_values", dv_back, inner_v, more)
    far_share = lax.ppermute(give_v[tokens:], "ctx", mirror)
    far_v = lax.ppermute(give_v[:tokens], "ctx", mirror)
    weight_at = tokens + 2 * rows
    weight_pair = (give_v[weight_at:].astype(F32) + far_share[2 * rows :].astype(F32)).astype(BF16)
    weight_sum = weight_pair.astype(F32)
    for step in range(1, batch):
        weight_sum += lax.ppermute(
            weight_pair, "batch", [(i, (i + step) % batch) for i in range(batch)]
        ).astype(F32)
    weight_sum, far_v = lax.optimization_barrier((weight_sum, far_v))
    glob_sum = give_v[tokens:weight_at].astype(F32) + far_share[: 2 * rows].astype(F32)
    share = jnp.concatenate([glob_sum, weight_sum], axis=0).astype(BF16)
    own_k, give_k = fold("fold_keys", dk_back, inner_k, 0)
    give_k, far_v = lax.optimization_barrier((give_k, far_v))
    far_k = lax.ppermute(give_k, "ctx", mirror)
    share, own_k = lax.optimization_barrier((share, own_k))
    if direct:
        pair = jnp.concatenate([share, flip(share, 1)], axis=0)
        totals = [pair] + [flip(pair, mask) for mask in (6, 2, 4)]
        masks = (0, 1, 6, 7, 2, 3, 4, 5)
    else:
        totals = [lax.all_gather(share, "ctx", axis=0, axis_index_groups=halves, tiled=True)]
        masks = tuple(range(half))
    attended = dot(attention_rows, output_weight, 1, 0).astype(BF16)

    grad_keys, grad_values, grad_weight = pl.pallas_call(
        functools.partial(finish_kernel, masks),
        name="finish",
        out_shape=(
            shape((tokens, width), BF16),
            shape((tokens, width), BF16),
            shape((width, model), F32),
        ),
        in_specs=[SMEM] + [VMEM] * (7 + len(totals)),
        out_specs=(VMEM,) * 3,
        scratch_shapes=[
            pltpu.VMEM((tokens, width), F32),
            pltpu.VMEM((glob, 2 * width), F32),
        ],
        compiler_params=params(24),
    )(here, glob_pos, own_k, own_v, far_k, far_v, from_low, from_high, *totals)
    return (
        attended[None],
        grad_queries[None],
        grad_keys[None],
        grad_values[None],
        grad_weight,
    )


def solution(mesh):
    in_specs = (
        P("batch", "ctx", None),
        P("batch", "ctx", None),
        P("batch", "ctx", None),
        P(),
        P("batch", "ctx", None),
        P("batch", "ctx", None),
        P("batch", None),
    )
    out_specs = (
        P("batch", "ctx", None),
        P("batch", "ctx", None),
        P("batch", "ctx", None),
        P("batch", "ctx", None),
        P(),
    )
    return jax.shard_map(shards, mesh=mesh, in_specs=in_specs, out_specs=out_specs, check_vma=False)
```

```python
import functools

import jax
import jax.numpy as jnp
from jax import lax
from jax.experimental import pallas as pl
from jax.experimental.pallas import tpu as pltpu
from jax.sharding import PartitionSpec as P

BLK = 64
HEADS = 4
RAND = 3
LANES = 128
MIB = 1024 * 1024
LOG2E = 1.4426950408889634
MASKS = (0, 6, 2, 4, 3, 5, 1, 7)

F32 = jnp.float32
BF16 = jnp.bfloat16
VMEM = pl.BlockSpec(memory_space=pltpu.VMEM)
SMEM = pl.BlockSpec(memory_space=pltpu.SMEM)


def params(mib):
    return pltpu.CompilerParams(vmem_limit_bytes=mib * MIB)


def dot(left, right, over_left, over_right):
    return lax.dot_general(
        left, right, (((over_left,), (over_right,)), ((), ())), preferred_element_type=F32
    )


def masks_of(half):
    return MASKS if half == len(MASKS) else tuple(range(half))


def member_of(here_ref, direct, half, j):
    return here_ref[1] ^ masks_of(half)[j] if direct else j


def rows_of(member, rows):
    if isinstance(member, int):
        return slice(member * rows, (member + 1) * rows)
    return pl.ds(pl.multiple_of(member * rows, rows), rows)


def ask_kernel(half, capacity, strides, here_ref, want_ref, pos_ref, k_ref, v_ref,
               send_ref, place_ref, v_out_ref, count_ref, list_ref):
    tokens, width = k_ref.shape
    glob = pos_ref.shape[1]
    query_blocks = tokens // BLK
    requests = query_blocks * RAND
    rows = glob // half
    lists = 2 * capacity
    me = here_ref[0]
    turn = here_ref[1]
    my_half = lax.div(me, half)
    for entry in range(2 * half):
        count_ref[entry] = 0
    for entry in range(half * lists):
        list_ref[entry] = -1

    def request(at, carry):
        wanted = want_ref[at]
        owner = lax.div(wanted, query_blocks)
        rank = jnp.minimum(count_ref[owner], capacity - 1)
        count_ref[owner] = count_ref[owner] + 1
        owner_half = lax.div(owner, half)
        member = owner - owner_half * half
        slot = jnp.where(owner_half == my_half, 0, capacity) + rank
        list_ref[member * lists + slot] = wanted - owner * query_blocks
        piece = member ^ turn
        piece = sum(jnp.where(piece == mask, j, 0) for j, mask in enumerate(masks_of(half)))
        for use, stride in enumerate(strides):
            place_ref[use * requests + at] = piece * stride + slot * BLK
        return carry

    lax.fori_loop(0, requests, request, 0)
    here = me * tokens + lax.broadcasted_iota(jnp.int32, (tokens, glob), 0)
    owned = jnp.where(here == pos_ref[...], 1.0, 0.0).astype(BF16)
    send_ref[:, :width] = dot(owned, k_ref[...], 0, 0).astype(BF16)
    send_ref[:, width : 2 * width] = dot(owned, v_ref[...], 0, 0).astype(BF16)
    v_out_ref[...] = v_ref[...]
    lane = lax.broadcasted_iota(jnp.int32, (rows, LANES), 1)
    for member in range(half):
        listed = jnp.full((rows, LANES), -1, jnp.int32)
        for slot in range(lists):
            listed = jnp.where(lane == slot, list_ref[member * lists + slot], listed)
        send_ref[member * rows : (member + 1) * rows, 2 * width :] = listed.astype(F32).astype(BF16)


def heard_kernel(half, got_ref, glob_ref, asked_ref):
    glob = got_ref.shape[0]
    rows = glob // half
    wide = glob_ref.shape[1]
    source = lax.broadcasted_iota(jnp.int32, (half, glob), 1)
    target = lax.broadcasted_iota(jnp.int32, (half, glob), 0)
    pick = jnp.where(source == target * rows, 1.0, 0.0).astype(BF16)
    asked_ref[...] = dot(pick, got_ref[:, wide:], 1, 0).astype(jnp.int32)
    source = lax.broadcasted_iota(jnp.int32, (rows, glob), 1)
    target = lax.broadcasted_iota(jnp.int32, (rows, glob), 0)
    total = jnp.where(lax.rem(source, rows) == target, 1.0, 0.0).astype(BF16)
    glob_ref[...] = dot(total, got_ref[:, :wide], 1, 0).astype(BF16)


def reply_kernel(half, capacity, direct, here_ref, asked_ref, k_ref, v_ref, mk_ref, mv_ref, glob_ref, mglob_ref,
                 *out_refs):
    tokens, width = k_ref.shape
    rows = glob_ref.shape[0]
    skip = 2 * capacity * BLK
    share = (glob_ref[...].astype(F32) + mglob_ref[...].astype(F32)).astype(BF16)
    for j, out_ref in enumerate(out_refs):
        member = member_of(here_ref, direct, half, j)
        for slot in range(2 * capacity):
            block = jnp.maximum(asked_ref[member, slot], 0)
            source = pl.ds(pl.multiple_of(block * BLK, BLK), BLK)
            target = slice(slot * BLK, (slot + 1) * BLK)
            own = slot < capacity
            out_ref[target, :width] = (k_ref if own else mk_ref)[source, :]
            out_ref[target, width:] = (v_ref if own else mv_ref)[source, :]
        out_ref[skip : skip + rows, :] = share


def attend_kernel(half, capacity, direct, place_ref, here_ref, q_ref, ga_ref, og_ref, k_ref, v_ref, low_ref, high_ref,
                  *refs):
    pieces, dk_pieces, dv_pieces = (refs[at : at + half] for at in range(0, 3 * half, half))
    inner_k_ref, inner_v_ref, elow_ref, ehigh_ref, att_ref, dq_ref = refs[3 * half : 3 * half + 6]
    pad_ref, kc_ref, vc_ref, acc_ref, gacc_ref, arr_ref, dk_out_ref, dv_out_ref = refs[3 * half + 6 :]
    tokens, width = q_ref.shape
    query_blocks = tokens // BLK
    head_size = width // HEADS
    scale = head_size ** (-0.5)
    win, local = 3 * BLK, (3 + RAND) * BLK
    requests = query_blocks * RAND
    pad_ref[:BLK] = low_ref[...]
    pad_ref[BLK : BLK + tokens, :width] = k_ref[...]
    pad_ref[BLK : BLK + tokens, width:] = v_ref[...]
    pad_ref[BLK + tokens :] = high_ref[...]
    skip = 2 * capacity * BLK
    rows = gacc_ref.shape[0] // half
    for j, piece in enumerate(pieces):
        stride = piece.shape[0]
        mine = slice(local + j * rows, local + (j + 1) * rows)
        arr_ref[j * stride : (j + 1) * stride] = piece[...]
        kc_ref[mine] = piece[skip : skip + rows, :width]
        vc_ref[mine] = piece[skip : skip + rows, width:]
    acc_ref[...] = jnp.zeros_like(acc_ref)
    gacc_ref[...] = jnp.zeros_like(gacc_ref)
    row_head = lax.broadcasted_iota(jnp.int32, (HEADS * BLK, width), 0) // BLK
    lane_head = lax.broadcasted_iota(jnp.int32, (HEADS * BLK, width), 1) // head_size
    mask = jnp.where(row_head == lane_head, 1.0, 0.0).astype(BF16)
    keep = jnp.where(row_head == lane_head, 1.0, 0.0)

    def by_head(rows):
        return jnp.concatenate([rows] * HEADS, axis=0) * mask

    def own_head(full):
        kept = full * keep
        return sum(kept[h * BLK : (h + 1) * BLK] for h in range(HEADS))

    def one_block(i, carry):
        base = pl.multiple_of(i * BLK, BLK)
        kc_ref[:win] = pad_ref[pl.ds(base, win), :width]
        vc_ref[:win] = pad_ref[pl.ds(base, win), width:]
        for j in range(RAND):
            slot = pl.ds(pl.multiple_of(place_ref[i * RAND + j], BLK), BLK)
            kc_ref[win + j * BLK : win + (j + 1) * BLK] = arr_ref[slot, :width]
            vc_ref[win + j * BLK : win + (j + 1) * BLK] = arr_ref[slot, width:]
        q_by_head = by_head(q_ref[pl.ds(base, BLK), :])
        ga_by_head = by_head(ga_ref[pl.ds(base, BLK), :])
        scores = dot(kc_ref[...], q_by_head, 1, 1) * (scale * LOG2E)
        expo = jnp.exp2(scores - jnp.max(scores, axis=0, keepdims=True))
        probs = expo * (1.0 / jnp.sum(expo, axis=0, keepdims=True))
        probs16 = probs.astype(BF16)
        dprobs = dot(vc_ref[...], ga_by_head, 1, 1)
        delta = jnp.sum(probs16.astype(F32) * dprobs, axis=0, keepdims=True)
        dscores = (probs * (dprobs - delta) * scale).astype(BF16)
        att_ref[pl.ds(base, BLK), :] = own_head(dot(probs16, vc_ref[...], 0, 0)).astype(BF16)
        dq_ref[pl.ds(base, BLK), :] = own_head(dot(dscores, kc_ref[...], 0, 0)).astype(BF16)
        for out_ref, part, terms in (
            (dv_out_ref, slice(width, 2 * width), dot(probs16, ga_by_head, 1, 0)),
            (dk_out_ref, slice(0, width), dot(dscores, q_by_head, 1, 0)),
        ):
            acc_ref[pl.ds(base, win), part] += terms[:win]
            gacc_ref[:, part] += terms[local:]
            for j in range(RAND):
                slot = place_ref[requests + i * RAND + j]
                out_ref[pl.ds(pl.multiple_of(slot, 16), BLK), :] = terms[
                    win + j * BLK : win + (j + 1) * BLK
                ].astype(BF16)
        return carry

    lax.fori_loop(0, query_blocks, one_block, 0, unroll=8)
    inner_k_ref[...] = acc_ref[BLK : BLK + tokens, :width]
    inner_v_ref[...] = acc_ref[BLK : BLK + tokens, width:]
    elow_ref[...] = acc_ref[:BLK].astype(BF16)
    ehigh_ref[...] = acc_ref[BLK + tokens :].astype(BF16)
    gacc_ref[:, 2 * width :] = dot(att_ref[...], og_ref[...], 0, 0)
    for j in range(half):
        dk_pieces[j][...] = dk_out_ref[j * skip : (j + 1) * skip]
        dv_pieces[j][:skip] = dv_out_ref[j * skip : (j + 1) * skip]
        member_rows = rows_of(member_of(here_ref, direct, half, j), rows)
        for part in range(gacc_ref.shape[1] // width):
            at = skip + part * rows
            mine = slice(j * rows, (j + 1) * rows) if part < 2 else member_rows
            dv_pieces[j][at : at + rows, :] = gacc_ref[
                mine, part * width : (part + 1) * width
            ].astype(BF16)


def fold_kernel(half, capacity, direct, here_ref, asked_ref, inner_ref, *refs):
    pieces = refs[:half]
    own_ref, give_ref, mirror_acc = refs[half:]
    tokens = own_ref.shape[0]
    skip = 2 * capacity * BLK
    own_ref[...] = inner_ref[...]
    mirror_acc[...] = jnp.zeros_like(mirror_acc)
    for j, piece in enumerate(pieces):
        member = member_of(here_ref, direct, half, j)
        for slot in range(2 * capacity):
            block = asked_ref[member, slot]
            acc_ref = own_ref if slot < capacity else mirror_acc
            at = slot * BLK

            @pl.when(block >= 0)
            def _():
                rows = pl.ds(pl.multiple_of(block * BLK, BLK), BLK)
                acc_ref[rows, :] += piece[at : at + BLK, :].astype(F32)

    give_ref[:tokens] = mirror_acc[...].astype(BF16)
    if pieces[0].shape[0] > skip:
        total = pieces[0][skip:, :].astype(F32)
        for piece in pieces[1:]:
            total += piece[skip:, :].astype(F32)
        give_ref[tokens:] = total.astype(BF16)


def finish_kernel(masks, here_ref, pos_ref, own_k_ref, own_v_ref, far_k_ref, far_v_ref, from_low_ref,
                  from_high_ref, *refs):
    dk_ref, dv_ref, weight_ref, acc_ref, glob_ref = refs[-5:]
    half = len(masks)
    tokens, width = dk_ref.shape
    glob = pos_ref.shape[1]
    rows = glob // half
    stride = sum(ref.shape[0] for ref in refs[:-5]) // half
    here = here_ref[0] * tokens + lax.broadcasted_iota(jnp.int32, (tokens, glob), 0)
    owned = jnp.where(here == pos_ref[...], 1.0, 0.0).astype(BF16)
    places = [(ref, at) for ref in refs[:-5] for at in range(0, ref.shape[0], stride)]
    for mask, (total_ref, first) in zip(masks, places):
        mine = rows_of(here_ref[1] ^ mask if len(refs) > 6 else mask, rows)
        for part in range(stride // rows):
            at = first + part * rows
            piece = total_ref[at : at + rows, :].astype(F32)
            if part < 2:
                glob_ref[mine, part * width : (part + 1) * width] = piece
            else:
                weight_ref[mine, (part - 2) * width : (part - 1) * width] = piece
    for part, own_ref, far_ref, out_ref in (
        (slice(0, width), own_k_ref, far_k_ref, dk_ref),
        (slice(width, 2 * width), own_v_ref, far_v_ref, dv_ref),
    ):
        acc_ref[...] = own_ref[...] + far_ref[:tokens].astype(F32) + dot(owned, glob_ref[:, part].astype(BF16), 1, 0)
        acc_ref[:BLK] += from_low_ref[:, part].astype(F32)
        acc_ref[tokens - BLK :] += from_high_ref[:, part].astype(F32)
        out_ref[...] = acc_ref[...].astype(BF16)


def shards(queries, keys, values, output_weight, output_grad, rand_blocks, glob_pos):
    q, k, v, og = queries[0], keys[0], values[0], output_grad[0]
    tokens, width = q.shape
    model = og.shape[1]
    glob = glob_pos.shape[1]
    query_blocks = tokens // BLK
    span = lax.axis_size("ctx")
    batch = lax.axis_size("batch")
    requests = query_blocks * RAND
    capacity = requests // span + 1
    half = span // 2
    rows = glob // half
    wide = 2 * width + model
    skip = 2 * capacity * BLK
    strides = (skip + -(-rows // 16) * 16, skip)
    more = rows * wide // width
    me = lax.axis_index("ctx").astype(jnp.int32)
    direct = half == 8
    here = jnp.stack([me, me % half if direct else jnp.zeros_like(me)])
    shape = jax.ShapeDtypeStruct
    forward = [(i, (i + 1) % span) for i in range(span)]
    backward = [(target, source) for source, target in forward]
    mirror = [(i, (i + half) % span) for i in range(span)]
    halves = [list(range(half)), list(range(half, span))]

    def swap(x):
        return lax.all_to_all(
            x, "ctx", split_axis=0, concat_axis=0, axis_index_groups=halves, tiled=True
        )

    def flip(x, mask):
        return lax.ppermute(x, "ctx", [(i, i ^ mask) for i in range(span)])

    def trade(pieces):
        if not direct:
            return [piece[0] for piece in jnp.split(swap(jnp.stack(pieces)), half)]
        return [pieces[0]] + [
            flip(pieces[j], mask) for j, mask in enumerate(masks_of(half)) if mask
        ]

    mirror_k = lax.ppermute(k, "ctx", mirror)
    send, places, v_after = pl.pallas_call(
        functools.partial(ask_kernel, half, capacity, strides),
        name="ask",
        out_shape=(
            shape((glob, 2 * width + LANES), BF16),
            shape((2 * requests,), jnp.int32),
            shape((tokens, width), BF16),
        ),
        in_specs=[SMEM, SMEM, VMEM, VMEM, VMEM],
        out_specs=(VMEM, SMEM, VMEM),
        scratch_shapes=[pltpu.SMEM((span,), jnp.int32), pltpu.SMEM((span * capacity,), jnp.int32)],
        compiler_params=params(60),
    )(here, rand_blocks.reshape(requests), glob_pos, k, v)
    got = swap(send)
    mirror_v = lax.ppermute(v_after, "ctx", mirror)
    key_value_edges = [
        jnp.concatenate([k[edge], v[edge]], axis=1)
        for edge in (slice(tokens - BLK, tokens), slice(0, BLK))
    ]
    low = lax.ppermute(key_value_edges[0], "ctx", forward)
    high = lax.ppermute(key_value_edges[1], "ctx", backward)
    grad_attn = dot(og, output_weight, 1, 1).astype(BF16)

    glob_here, asked = pl.pallas_call(
        functools.partial(heard_kernel, half),
        name="heard",
        out_shape=(shape((rows, 2 * width), BF16), shape((half, LANES), jnp.int32)),
        in_specs=[VMEM],
        out_specs=(VMEM,) * 2,
        compiler_params=params(16),
    )(got)
    glob_there = lax.ppermute(glob_here, "ctx", mirror)
    reply = pl.pallas_call(
        functools.partial(reply_kernel, half, capacity, direct),
        name="reply",
        out_shape=[shape((strides[0], 2 * width), BF16)] * half,
        in_specs=[SMEM, SMEM] + [VMEM] * 6,
        out_specs=[VMEM] * half,
        compiler_params=params(16),
    )(here, asked, k, v, mirror_k, mirror_v, glob_here, glob_there)
    reply, low, high = lax.optimization_barrier((reply, low, high))
    arrived = trade(reply)

    block = (3 + RAND) * BLK + glob
    *gives, inner_k, inner_v, edge_low, edge_high, attention_rows, grad_queries = pl.pallas_call(
        functools.partial(attend_kernel, half, capacity, direct),
        name="attend",
        out_shape=[shape((skip, width), BF16)] * half
        + [shape((skip + more, width), BF16)] * half
        + [
            shape((tokens, width), F32),
            shape((tokens, width), F32),
            shape((BLK, 2 * width), BF16),
            shape((BLK, 2 * width), BF16),
            shape((tokens, width), BF16),
            shape((tokens, width), BF16),
        ],
        in_specs=[SMEM, SMEM] + [VMEM] * (7 + half),
        out_specs=[VMEM] * (2 * half + 6),
        scratch_shapes=[
            pltpu.VMEM((tokens + 2 * BLK, 2 * width), BF16),
            pltpu.VMEM((block, width), BF16),
            pltpu.VMEM((block, width), BF16),
            pltpu.VMEM((tokens + 2 * BLK, 2 * width), F32),
            pltpu.VMEM((glob, wide), F32),
            pltpu.VMEM((half * strides[0], 2 * width), BF16),
            pltpu.VMEM((half * skip, width), BF16),
            pltpu.VMEM((half * skip, width), BF16),
        ],
        compiler_params=params(32),
    )(places, here, q, grad_attn, og, k, v, low, high, *arrived)

    from_high = lax.ppermute(edge_low, "ctx", backward)
    from_low = lax.ppermute(edge_high, "ctx", forward)
    dv_back = trade(gives[half:])
    dk_back = trade(gives[:half])

    def fold(name, back, inner, more):
        return pl.pallas_call(
            functools.partial(fold_kernel, half, capacity, direct),
            name=name,
            out_shape=(shape((tokens, width), F32), shape((tokens + more, width), BF16)),
            in_specs=[SMEM, SMEM, VMEM] + [VMEM] * half,
            out_specs=(VMEM,) * 2,
            scratch_shapes=[pltpu.VMEM((tokens, width), F32)],
            compiler_params=params(16),
        )(here, asked, inner, *back)

    own_v, give_v = fold("fold_values", dv_back, inner_v, more)
    far_share = lax.ppermute(give_v[tokens:], "ctx", mirror)
    far_v = lax.ppermute(give_v[:tokens], "ctx", mirror)
    weight_at = tokens + 2 * rows
    weight_pair = (give_v[weight_at:].astype(F32) + far_share[2 * rows :].astype(F32)).astype(BF16)
    weight_sum = weight_pair.astype(F32)
    for step in range(1, batch):
        weight_sum += lax.ppermute(
            weight_pair, "batch", [(i, (i + step) % batch) for i in range(batch)]
        ).astype(F32)
    weight_sum, far_v = lax.optimization_barrier((weight_sum, far_v))
    glob_sum = give_v[tokens:weight_at].astype(F32) + far_share[: 2 * rows].astype(F32)
    share = jnp.concatenate([glob_sum, weight_sum], axis=0).astype(BF16)
    own_k, give_k = fold("fold_keys", dk_back, inner_k, 0)
    give_k, far_v = lax.optimization_barrier((give_k, far_v))
    far_k = lax.ppermute(give_k, "ctx", mirror)
    share, own_k = lax.optimization_barrier((share, own_k))
    if direct:
        pair = jnp.concatenate([share, flip(share, 1)], axis=0)
        totals = [pair] + [flip(pair, mask) for mask in (2, 4, 6)]
        masks = (0, 1, 2, 3, 4, 5, 6, 7)
    else:
        totals = [lax.all_gather(share, "ctx", axis=0, axis_index_groups=halves, tiled=True)]
        masks = tuple(range(half))
    attended = dot(attention_rows, output_weight, 1, 0).astype(BF16)

    grad_keys, grad_values, grad_weight = pl.pallas_call(
        functools.partial(finish_kernel, masks),
        name="finish",
        out_shape=(
            shape((tokens, width), BF16),
            shape((tokens, width), BF16),
            shape((width, model), F32),
        ),
        in_specs=[SMEM] + [VMEM] * (7 + len(totals)),
        out_specs=(VMEM,) * 3,
        scratch_shapes=[
            pltpu.VMEM((tokens, width), F32),
            pltpu.VMEM((glob, 2 * width), F32),
        ],
        compiler_params=params(24),
    )(here, glob_pos, own_k, own_v, far_k, far_v, from_low, from_high, *totals)
    return (
        attended[None],
        grad_queries[None],
        grad_keys[None],
        grad_values[None],
        grad_weight,
    )


def solution(mesh):
    in_specs = (
        P("batch", "ctx", None),
        P("batch", "ctx", None),
        P("batch", "ctx", None),
        P(),
        P("batch", "ctx", None),
        P("batch", "ctx", None),
        P("batch", None),
    )
    out_specs = (
        P("batch", "ctx", None),
        P("batch", "ctx", None),
        P("batch", "ctx", None),
        P("batch", "ctx", None),
        P(),
    )
    return jax.shard_map(shards, mesh=mesh, in_specs=in_specs, out_specs=out_specs, check_vma=False)
```

```python
import functools

import jax
import jax.numpy as jnp
from jax import lax
from jax.experimental import pallas as pl
from jax.experimental.pallas import tpu as pltpu
from jax.sharding import PartitionSpec as P

BLK = 64
HEADS = 4
RAND = 3
LANES = 128
MIB = 1024 * 1024
LOG2E = 1.4426950408889634
MASKS = (0, 6, 2, 4, 3, 5, 1, 7)

F32 = jnp.float32
BF16 = jnp.bfloat16
VMEM = pl.BlockSpec(memory_space=pltpu.VMEM)
SMEM = pl.BlockSpec(memory_space=pltpu.SMEM)


def params(mib):
    return pltpu.CompilerParams(vmem_limit_bytes=mib * MIB)


def dot(left, right, over_left, over_right):
    return lax.dot_general(
        left, right, (((over_left,), (over_right,)), ((), ())), preferred_element_type=F32
    )


def masks_of(half):
    return MASKS if half == len(MASKS) else tuple(range(half))


def member_of(here_ref, direct, half, j):
    return here_ref[1] ^ masks_of(half)[j] if direct else j


def rows_of(member, rows):
    if isinstance(member, int):
        return slice(member * rows, (member + 1) * rows)
    return pl.ds(pl.multiple_of(member * rows, rows), rows)


def ask_kernel(half, capacity, strides, here_ref, want_ref, pos_ref, k_ref, v_ref,
               send_ref, place_ref, v_out_ref, count_ref, list_ref):
    tokens, width = k_ref.shape
    glob = pos_ref.shape[1]
    query_blocks = tokens // BLK
    requests = query_blocks * RAND
    rows = glob // half
    lists = 2 * capacity
    me = here_ref[0]
    turn = here_ref[1]
    my_half = lax.div(me, half)
    for entry in range(2 * half):
        count_ref[entry] = 0
    for entry in range(half * lists):
        list_ref[entry] = -1

    def request(at, carry):
        wanted = want_ref[at]
        owner = lax.div(wanted, query_blocks)
        rank = jnp.minimum(count_ref[owner], capacity - 1)
        count_ref[owner] = count_ref[owner] + 1
        owner_half = lax.div(owner, half)
        member = owner - owner_half * half
        slot = jnp.where(owner_half == my_half, 0, capacity) + rank
        list_ref[member * lists + slot] = wanted - owner * query_blocks
        piece = member ^ turn
        piece = sum(jnp.where(piece == mask, j, 0) for j, mask in enumerate(masks_of(half)))
        for use, stride in enumerate(strides):
            place_ref[use * requests + at] = piece * stride + slot * BLK
        return carry

    lax.fori_loop(0, requests, request, 0)
    here = me * tokens + lax.broadcasted_iota(jnp.int32, (tokens, glob), 0)
    owned = jnp.where(here == pos_ref[...], 1.0, 0.0).astype(BF16)
    send_ref[:, :width] = dot(owned, k_ref[...], 0, 0).astype(BF16)
    send_ref[:, width : 2 * width] = dot(owned, v_ref[...], 0, 0).astype(BF16)
    v_out_ref[...] = v_ref[...]
    lane = lax.broadcasted_iota(jnp.int32, (rows, LANES), 1)
    for member in range(half):
        listed = jnp.full((rows, LANES), -1, jnp.int32)
        for slot in range(lists):
            listed = jnp.where(lane == slot, list_ref[member * lists + slot], listed)
        send_ref[member * rows : (member + 1) * rows, 2 * width :] = listed.astype(F32).astype(BF16)


def heard_kernel(half, got_ref, glob_ref, asked_ref):
    glob = got_ref.shape[0]
    rows = glob // half
    wide = glob_ref.shape[1]
    source = lax.broadcasted_iota(jnp.int32, (half, glob), 1)
    target = lax.broadcasted_iota(jnp.int32, (half, glob), 0)
    pick = jnp.where(source == target * rows, 1.0, 0.0).astype(BF16)
    asked_ref[...] = dot(pick, got_ref[:, wide:], 1, 0).astype(jnp.int32)
    source = lax.broadcasted_iota(jnp.int32, (rows, glob), 1)
    target = lax.broadcasted_iota(jnp.int32, (rows, glob), 0)
    total = jnp.where(lax.rem(source, rows) == target, 1.0, 0.0).astype(BF16)
    glob_ref[...] = dot(total, got_ref[:, :wide], 1, 0).astype(BF16)


def reply_kernel(half, capacity, direct, here_ref, asked_ref, k_ref, v_ref, mk_ref, mv_ref, glob_ref, mglob_ref,
                 *out_refs):
    tokens, width = k_ref.shape
    rows = glob_ref.shape[0]
    skip = 2 * capacity * BLK
    share = (glob_ref[...].astype(F32) + mglob_ref[...].astype(F32)).astype(BF16)
    for j, out_ref in enumerate(out_refs):
        member = member_of(here_ref, direct, half, j)
        for slot in range(2 * capacity):
            block = jnp.maximum(asked_ref[member, slot], 0)
            source = pl.ds(pl.multiple_of(block * BLK, BLK), BLK)
            target = slice(slot * BLK, (slot + 1) * BLK)
            own = slot < capacity
            out_ref[target, :width] = (k_ref if own else mk_ref)[source, :]
            out_ref[target, width:] = (v_ref if own else mv_ref)[source, :]
        out_ref[skip : skip + rows, :] = share


def attend_kernel(half, capacity, direct, place_ref, here_ref, q_ref, ga_ref, og_ref, k_ref, v_ref, low_ref, high_ref,
                  *refs):
    pieces, dk_pieces, dv_pieces = (refs[at : at + half] for at in range(0, 3 * half, half))
    inner_k_ref, inner_v_ref, elow_ref, ehigh_ref, att_ref, dq_ref = refs[3 * half : 3 * half + 6]
    pad_ref, kc_ref, vc_ref, acc_ref, gacc_ref, arr_ref, dk_out_ref, dv_out_ref = refs[3 * half + 6 :]
    tokens, width = q_ref.shape
    query_blocks = tokens // BLK
    head_size = width // HEADS
    scale = head_size ** (-0.5)
    win, local = 3 * BLK, (3 + RAND) * BLK
    requests = query_blocks * RAND
    pad_ref[:BLK] = low_ref[...]
    pad_ref[BLK : BLK + tokens, :width] = k_ref[...]
    pad_ref[BLK : BLK + tokens, width:] = v_ref[...]
    pad_ref[BLK + tokens :] = high_ref[...]
    skip = 2 * capacity * BLK
    rows = gacc_ref.shape[0] // half
    for j, piece in enumerate(pieces):
        stride = piece.shape[0]
        mine = slice(local + j * rows, local + (j + 1) * rows)
        arr_ref[j * stride : (j + 1) * stride] = piece[...]
        kc_ref[mine] = piece[skip : skip + rows, :width]
        vc_ref[mine] = piece[skip : skip + rows, width:]
    acc_ref[...] = jnp.zeros_like(acc_ref)
    gacc_ref[...] = jnp.zeros_like(gacc_ref)
    row_head = lax.broadcasted_iota(jnp.int32, (HEADS * BLK, width), 0) // BLK
    lane_head = lax.broadcasted_iota(jnp.int32, (HEADS * BLK, width), 1) // head_size
    mask = jnp.where(row_head == lane_head, 1.0, 0.0).astype(BF16)
    keep = jnp.where(row_head == lane_head, 1.0, 0.0)

    def by_head(rows):
        return jnp.concatenate([rows] * HEADS, axis=0) * mask

    def own_head(full):
        kept = full * keep
        return sum(kept[h * BLK : (h + 1) * BLK] for h in range(HEADS))

    def one_block(i, carry):
        base = pl.multiple_of(i * BLK, BLK)
        kc_ref[:win] = pad_ref[pl.ds(base, win), :width]
        vc_ref[:win] = pad_ref[pl.ds(base, win), width:]
        for j in range(RAND):
            slot = pl.ds(pl.multiple_of(place_ref[i * RAND + j], 16), BLK)
            kc_ref[win + j * BLK : win + (j + 1) * BLK] = arr_ref[slot, :width]
            vc_ref[win + j * BLK : win + (j + 1) * BLK] = arr_ref[slot, width:]
        q_by_head = by_head(q_ref[pl.ds(base, BLK), :])
        ga_by_head = by_head(ga_ref[pl.ds(base, BLK), :])
        scores = dot(kc_ref[...], q_by_head, 1, 1) * (scale * LOG2E)
        expo = jnp.exp2(scores - jnp.max(scores, axis=0, keepdims=True))
        probs = expo * (1.0 / jnp.sum(expo, axis=0, keepdims=True))
        probs16 = probs.astype(BF16)
        dprobs = dot(vc_ref[...], ga_by_head, 1, 1)
        delta = jnp.sum(probs16.astype(F32) * dprobs, axis=0, keepdims=True)
        dscores = (probs * (dprobs - delta) * scale).astype(BF16)
        att_ref[pl.ds(base, BLK), :] = own_head(dot(probs16, vc_ref[...], 0, 0)).astype(BF16)
        dq_ref[pl.ds(base, BLK), :] = own_head(dot(dscores, kc_ref[...], 0, 0)).astype(BF16)
        for out_ref, part, terms in (
            (dv_out_ref, slice(width, 2 * width), dot(probs16, ga_by_head, 1, 0)),
            (dk_out_ref, slice(0, width), dot(dscores, q_by_head, 1, 0)),
        ):
            acc_ref[pl.ds(base, win), part] += terms[:win]
            gacc_ref[:, part] += terms[local:]
            for j in range(RAND):
                slot = place_ref[requests + i * RAND + j]
                out_ref[pl.ds(pl.multiple_of(slot, 16), BLK), :] = terms[
                    win + j * BLK : win + (j + 1) * BLK
                ].astype(BF16)
        return carry

    lax.fori_loop(0, query_blocks, one_block, 0, unroll=8)
    inner_k_ref[...] = acc_ref[BLK : BLK + tokens, :width]
    inner_v_ref[...] = acc_ref[BLK : BLK + tokens, width:]
    elow_ref[...] = acc_ref[:BLK].astype(BF16)
    ehigh_ref[...] = acc_ref[BLK + tokens :].astype(BF16)
    gacc_ref[:, 2 * width :] = dot(att_ref[...], og_ref[...], 0, 0)
    for j in range(half):
        dk_pieces[j][...] = dk_out_ref[j * skip : (j + 1) * skip]
        dv_pieces[j][:skip] = dv_out_ref[j * skip : (j + 1) * skip]
        member_rows = rows_of(member_of(here_ref, direct, half, j), rows)
        for part in range(gacc_ref.shape[1] // width):
            at = skip + part * rows
            mine = slice(j * rows, (j + 1) * rows) if part < 2 else member_rows
            dv_pieces[j][at : at + rows, :] = gacc_ref[
                mine, part * width : (part + 1) * width
            ].astype(BF16)


def fold_kernel(half, capacity, direct, here_ref, asked_ref, inner_ref, *refs):
    pieces = refs[:half]
    own_ref, give_ref, mirror_acc = refs[half:]
    tokens = own_ref.shape[0]
    skip = 2 * capacity * BLK
    own_ref[...] = inner_ref[...]
    mirror_acc[...] = jnp.zeros_like(mirror_acc)
    for j, piece in enumerate(pieces):
        member = member_of(here_ref, direct, half, j)
        for slot in range(2 * capacity):
            block = asked_ref[member, slot]
            acc_ref = own_ref if slot < capacity else mirror_acc
            at = slot * BLK

            @pl.when(block >= 0)
            def _():
                rows = pl.ds(pl.multiple_of(block * BLK, BLK), BLK)
                acc_ref[rows, :] += piece[at : at + BLK, :].astype(F32)

    give_ref[:tokens] = mirror_acc[...].astype(BF16)
    if pieces[0].shape[0] > skip:
        total = pieces[0][skip:, :].astype(F32)
        for piece in pieces[1:]:
            total += piece[skip:, :].astype(F32)
        give_ref[tokens:] = total.astype(BF16)


def finish_kernel(masks, here_ref, pos_ref, own_k_ref, own_v_ref, far_k_ref, far_v_ref, from_low_ref,
                  from_high_ref, *refs):
    dk_ref, dv_ref, weight_ref, acc_ref, glob_ref = refs[-5:]
    half = len(masks)
    tokens, width = dk_ref.shape
    glob = pos_ref.shape[1]
    rows = glob // half
    stride = sum(ref.shape[0] for ref in refs[:-5]) // half
    here = here_ref[0] * tokens + lax.broadcasted_iota(jnp.int32, (tokens, glob), 0)
    owned = jnp.where(here == pos_ref[...], 1.0, 0.0).astype(BF16)
    places = [(ref, at) for ref in refs[:-5] for at in range(0, ref.shape[0], stride)]
    for mask, (total_ref, first) in zip(masks, places):
        mine = rows_of(here_ref[1] ^ mask if len(refs) > 6 else mask, rows)
        for part in range(stride // rows):
            at = first + part * rows
            piece = total_ref[at : at + rows, :].astype(F32)
            if part < 2:
                glob_ref[mine, part * width : (part + 1) * width] = piece
            else:
                weight_ref[mine, (part - 2) * width : (part - 1) * width] = piece
    for part, own_ref, far_ref, out_ref in (
        (slice(0, width), own_k_ref, far_k_ref, dk_ref),
        (slice(width, 2 * width), own_v_ref, far_v_ref, dv_ref),
    ):
        acc_ref[...] = own_ref[...] + far_ref[:tokens].astype(F32) + dot(owned, glob_ref[:, part].astype(BF16), 1, 0)
        acc_ref[:BLK] += from_low_ref[:, part].astype(F32)
        acc_ref[tokens - BLK :] += from_high_ref[:, part].astype(F32)
        out_ref[...] = acc_ref[...].astype(BF16)


def shards(queries, keys, values, output_weight, output_grad, rand_blocks, glob_pos):
    q, k, v, og = queries[0], keys[0], values[0], output_grad[0]
    tokens, width = q.shape
    model = og.shape[1]
    glob = glob_pos.shape[1]
    query_blocks = tokens // BLK
    span = lax.axis_size("ctx")
    batch = lax.axis_size("batch")
    requests = query_blocks * RAND
    capacity = requests // span + 1
    half = span // 2
    rows = glob // half
    wide = 2 * width + model
    skip = 2 * capacity * BLK
    strides = (skip + -(-rows // 16) * 16, skip)
    more = rows * wide // width
    me = lax.axis_index("ctx").astype(jnp.int32)
    direct = half == 8
    here = jnp.stack([me, me % half if direct else jnp.zeros_like(me)])
    shape = jax.ShapeDtypeStruct
    forward = [(i, (i + 1) % span) for i in range(span)]
    backward = [(target, source) for source, target in forward]
    mirror = [(i, (i + half) % span) for i in range(span)]
    halves = [list(range(half)), list(range(half, span))]

    def swap(x):
        return lax.all_to_all(
            x, "ctx", split_axis=0, concat_axis=0, axis_index_groups=halves, tiled=True
        )

    def flip(x, mask):
        return lax.ppermute(x, "ctx", [(i, i ^ mask) for i in range(span)])

    def trade(pieces):
        if not direct:
            return [piece[0] for piece in jnp.split(swap(jnp.stack(pieces)), half)]
        return [pieces[0]] + [
            flip(pieces[j], mask) for j, mask in enumerate(masks_of(half)) if mask
        ]

    mirror_k = lax.ppermute(k, "ctx", mirror)
    send, places, v_after = pl.pallas_call(
        functools.partial(ask_kernel, half, capacity, strides),
        name="ask",
        out_shape=(
            shape((glob, 2 * width + LANES), BF16),
            shape((2 * requests,), jnp.int32),
            shape((tokens, width), BF16),
        ),
        in_specs=[SMEM, SMEM, VMEM, VMEM, VMEM],
        out_specs=(VMEM, SMEM, VMEM),
        scratch_shapes=[pltpu.SMEM((span,), jnp.int32), pltpu.SMEM((span * capacity,), jnp.int32)],
        compiler_params=params(60),
    )(here, rand_blocks.reshape(requests), glob_pos, k, v)
    got = swap(send)
    mirror_v = lax.ppermute(v_after, "ctx", mirror)
    key_value_edges = [
        jnp.concatenate([k[edge], v[edge]], axis=1)
        for edge in (slice(tokens - BLK, tokens), slice(0, BLK))
    ]
    low = lax.ppermute(key_value_edges[0], "ctx", forward)
    high = lax.ppermute(key_value_edges[1], "ctx", backward)
    grad_attn = dot(og, output_weight, 1, 1).astype(BF16)

    glob_here, asked = pl.pallas_call(
        functools.partial(heard_kernel, half),
        name="heard",
        out_shape=(shape((rows, 2 * width), BF16), shape((half, LANES), jnp.int32)),
        in_specs=[VMEM],
        out_specs=(VMEM,) * 2,
        compiler_params=params(16),
    )(got)
    glob_there = lax.ppermute(glob_here, "ctx", mirror)
    reply = pl.pallas_call(
        functools.partial(reply_kernel, half, capacity, direct),
        name="reply",
        out_shape=[shape((strides[0], 2 * width), BF16)] * half,
        in_specs=[SMEM, SMEM] + [VMEM] * 6,
        out_specs=[VMEM] * half,
        compiler_params=params(16),
    )(here, asked, k, v, mirror_k, mirror_v, glob_here, glob_there)
    reply, low, high = lax.optimization_barrier((reply, low, high))
    arrived = trade(reply)

    block = (3 + RAND) * BLK + glob
    *gives, inner_k, inner_v, edge_low, edge_high, attention_rows, grad_queries = pl.pallas_call(
        functools.partial(attend_kernel, half, capacity, direct),
        name="attend",
        out_shape=[shape((skip, width), BF16)] * half
        + [shape((skip + more, width), BF16)] * half
        + [
            shape((tokens, width), F32),
            shape((tokens, width), F32),
            shape((BLK, 2 * width), BF16),
            shape((BLK, 2 * width), BF16),
            shape((tokens, width), BF16),
            shape((tokens, width), BF16),
        ],
        in_specs=[SMEM, SMEM] + [VMEM] * (7 + half),
        out_specs=[VMEM] * (2 * half + 6),
        scratch_shapes=[
            pltpu.VMEM((tokens + 2 * BLK, 2 * width), BF16),
            pltpu.VMEM((block, width), BF16),
            pltpu.VMEM((block, width), BF16),
            pltpu.VMEM((tokens + 2 * BLK, 2 * width), F32),
            pltpu.VMEM((glob, wide), F32),
            pltpu.VMEM((half * strides[0], 2 * width), BF16),
            pltpu.VMEM((half * skip, width), BF16),
            pltpu.VMEM((half * skip, width), BF16),
        ],
        compiler_params=params(32),
    )(places, here, q, grad_attn, og, k, v, low, high, *arrived)

    from_high = lax.ppermute(edge_low, "ctx", backward)
    from_low = lax.ppermute(edge_high, "ctx", forward)
    dv_back = trade(gives[half:])
    dk_back = trade(gives[:half])

    def fold(name, back, inner, more):
        return pl.pallas_call(
            functools.partial(fold_kernel, half, capacity, direct),
            name=name,
            out_shape=(shape((tokens, width), F32), shape((tokens + more, width), BF16)),
            in_specs=[SMEM, SMEM, VMEM] + [VMEM] * half,
            out_specs=(VMEM,) * 2,
            scratch_shapes=[pltpu.VMEM((tokens, width), F32)],
            compiler_params=params(16),
        )(here, asked, inner, *back)

    own_v, give_v = fold("fold_values", dv_back, inner_v, more)
    far_share = lax.ppermute(give_v[tokens:], "ctx", mirror)
    far_v = lax.ppermute(give_v[:tokens], "ctx", mirror)
    weight_at = tokens + 2 * rows
    weight_pair = (give_v[weight_at:].astype(F32) + far_share[2 * rows :].astype(F32)).astype(BF16)
    weight_sum = weight_pair.astype(F32)
    for step in range(1, batch):
        weight_sum += lax.ppermute(
            weight_pair, "batch", [(i, (i + step) % batch) for i in range(batch)]
        ).astype(F32)
    weight_sum, far_v = lax.optimization_barrier((weight_sum, far_v))
    glob_sum = give_v[tokens:weight_at].astype(F32) + far_share[: 2 * rows].astype(F32)
    share = jnp.concatenate([glob_sum, weight_sum], axis=0).astype(BF16)
    own_k, give_k = fold("fold_keys", dk_back, inner_k, 0)
    give_k, far_v = lax.optimization_barrier((give_k, far_v))
    far_k = lax.ppermute(give_k, "ctx", mirror)
    share, own_k, from_high, from_low = lax.optimization_barrier(
        (share, own_k, from_high, from_low)
    )
    if direct:
        pair = jnp.concatenate([share, flip(share, 1)], axis=0)
        totals = [pair] + [flip(pair, mask) for mask in (2, 4, 6)]
        masks = (0, 1, 2, 3, 4, 5, 6, 7)
    else:
        totals = [lax.all_gather(share, "ctx", axis=0, axis_index_groups=halves, tiled=True)]
        masks = tuple(range(half))
    attended = dot(attention_rows, output_weight, 1, 0).astype(BF16)

    grad_keys, grad_values, grad_weight = pl.pallas_call(
        functools.partial(finish_kernel, masks),
        name="finish",
        out_shape=(
            shape((tokens, width), BF16),
            shape((tokens, width), BF16),
            shape((width, model), F32),
        ),
        in_specs=[SMEM] + [VMEM] * (7 + len(totals)),
        out_specs=(VMEM,) * 3,
        scratch_shapes=[
            pltpu.VMEM((tokens, width), F32),
            pltpu.VMEM((glob, 2 * width), F32),
        ],
        compiler_params=params(24),
    )(here, glob_pos, own_k, own_v, far_k, far_v, from_low, from_high, *totals)
    return (
        attended[None],
        grad_queries[None],
        grad_keys[None],
        grad_values[None],
        grad_weight,
    )


def solution(mesh):
    in_specs = (
        P("batch", "ctx", None),
        P("batch", "ctx", None),
        P("batch", "ctx", None),
        P(),
        P("batch", "ctx", None),
        P("batch", "ctx", None),
        P("batch", None),
    )
    out_specs = (
        P("batch", "ctx", None),
        P("batch", "ctx", None),
        P("batch", "ctx", None),
        P("batch", "ctx", None),
        P(),
    )
    return jax.shard_map(shards, mesh=mesh, in_specs=in_specs, out_specs=out_specs, check_vma=False)
```
